32 devices in a mesh: member: 2 (over y), lon: 4 (over z), lat: 2 (over x), lev: 2 (over core).
Axes of the slice: x: 2, y: 2, z: 4, core: 2. Of those that a mesh axis runs over, the one named last changes fastest.
Arguments:
- trajectory: bfloat16 [4, 3, 2, 512, 512], P('member', None, 'lev', 'lat', 'lon'), parts along dimension 0, may hold values from -6 to 6
- block_weights: float32 [8, 8], replicated, may hold values from 0.005 to 0.03
- wind_speed: float32 [2, 64, 64], P('lev', 'lat', 'lon'), may hold values from 0.05 to 0.45
- settling: float32 [3, 2], replicated, may hold values from 0.02 to 0.25
- source_mask: int32 [64, 64], P('lat', 'lon'), may hold values 0 or 1
- obs_columns: int32 [128, 32], P('member'), parts along dimension 0, may hold values from 0 to 63
- obs_values: float32 [4, 64, 32], P('member'), parts along dimension 0, may hold values from -6 to 6
- obs_weights: float32 [4, 64, 32], P('member'), parts along dimension 0, may hold values from 0.3 to 3
Outputs:
- analysis: bfloat16 [4, 3, 2, 512, 512], P('member', None, 'lev', 'lat', 'lon'), parts along dimension 0
- correction: float32 [4, 3, 2, 64, 64], P('member', None, 'lev', 'lat', 'lon'), parts along dimension 0
The draws below stay inside these ranges and needn't reach their ends.
There are 2 independent parts, one for each index of `member`. The reference program is written for one: setup_inputs(seed, part) draws one part's arguments, and reference() takes and returns one part's arrays. A program takes and returns all parts, laid end to end along the dimension named above; an argument that names none is the same for every part. Nothing has to cross between parts.
All inputs are finite; a program needn't handle non-finite values. No bound on the sum of `source_mask` on one device may be relied on, other than what follows from the above.
Results may differ from the reference program's by a relative error of at most 0.001.
Values sent between devices are 32-bit elements; how exact they have to be, the bound alone decides.
No kernel may reach another device: no remote copies, remote signals or barrier semaphores. Data moves between devices by JAX's collectives and lax.ppermute only.
A program may use at most 64 MiB of HBM per device.

```python
import math
import jax
import jax.numpy as jnp
from jax import lax

OBS = 32
BINS = 3
SLOTS = 2
BLOCK = 8
STEPS = 4
SWEEPS = 2
NLON = 512
NLAT = 512
NLEV = 2
CLON = 64
CLAT = 64


def place_ends(drawn, stream_key, low, high):
    spot = [jax.random.randint(jax.random.fold_in(stream_key, axis), (), 0, length) for axis, length in enumerate(drawn.shape)]
    longest = drawn.shape.index(max(drawn.shape))
    neighbour = spot[:longest] + [(spot[longest] + 1) % drawn.shape[longest]] + spot[longest + 1:]
    return drawn.at[tuple(spot)].set(low).at[tuple(neighbour)].set(high)


def steps_of(stream_key, dims, shards, smallest, high):
    loudness, own = 1.0, jax.random.fold_in(stream_key, 6)
    for dim, parts in shards:
        draws = jnp.exp(jax.random.uniform(jax.random.fold_in(own, dim), (parts,), jnp.float32, smallest / len(shards), high / len(shards)))
        loudness = loudness * jnp.repeat(draws, dims[dim] // parts).reshape([-1 if axis == dim else 1 for axis in range(len(dims))])
    return loudness


def bell_draw(own_key, shape, scale, limit, split=(), kind=jnp.bfloat16):
    loudness = steps_of(own_key, shape, split, -0.22, 0.18) if split else 1.0
    drawn = jax.random.normal(own_key, shape, jnp.float32) * scale * loudness
    return jnp.minimum(jnp.maximum(drawn, -limit), limit).astype(kind)


def setup_inputs(seed: int = 0, part: int = 0) -> dict:
    keys = jax.random.split(jax.random.key(seed), 9)
    part_keys = jax.random.split(jax.random.fold_in(keys[8], part), 9)
    trajectory = bell_draw(part_keys[0], (SLOTS, BINS, NLEV, NLAT, NLON), 1.0, 6.0, ((2, 2), (3, 2), (4, 4)))
    block_weights = jnp.clip(jax.random.uniform(keys[1], (BLOCK, BLOCK), jnp.float32, 0.005, 0.03), 0.005, 0.03)
    wind_speed = jnp.clip(0.05 + 0.39999999 * jax.random.uniform(keys[2], (NLEV, CLAT, CLON), jnp.float32) ** steps_of(keys[2], (NLEV, CLAT, CLON), ((0, 2), (1, 2), (2, 4)), -0.2, 0.2), 0.05, 0.45)
    settling = jnp.clip(jnp.exp(jax.random.uniform(keys[3], (BINS, NLEV), jnp.float32, math.log(0.02), math.log(0.25))), 0.02, 0.25)
    source_mask = place_ends((jax.random.randint(keys[4], (CLAT, CLON), 0, 2) < 1).astype(jnp.int32), jax.random.fold_in(keys[4], 1), 0, 1)
    obs_columns = place_ends(jax.random.randint(part_keys[5], (CLAT, OBS), 0, CLON), jax.random.fold_in(part_keys[5], 1), 0, CLON - 1).astype(jnp.int32)
    obs_values = bell_draw(part_keys[6], (SLOTS, CLAT, OBS), 1.0, 6.0, (), jnp.float32)
    obs_weights = jnp.clip(jnp.exp(jax.random.uniform(part_keys[7], (SLOTS, CLAT, OBS), jnp.float32, math.log(0.3), math.log(3.0))), 0.3, 3.0)
    return dict(trajectory=trajectory, block_weights=block_weights, wind_speed=wind_speed, settling=settling, source_mask=source_mask, obs_columns=obs_columns, obs_values=obs_values, obs_weights=obs_weights)


diffusion = 0.05
background = 0.1
step_length = 4.0


def lat_terms(values):
    zero_row = jnp.zeros_like(values[:, :, :, :1])
    north_cells = jnp.concatenate([values[:, :, :, 1:], zero_row], axis=3)
    south_cells = jnp.concatenate([zero_row, values[:, :, :, :-1]], axis=3)
    return diffusion * (north_cells + south_cells - 2.0 * values)


def forward_step(values, wind_speed, settling):
    mass_flux = wind_speed * values
    west_cells = jnp.roll(values, 1, 4)
    east_cells = jnp.roll(values, -1, 4)
    flux_west = jnp.roll(mass_flux, 1, 4)
    sinking = settling[None, :, :, None, None] * values
    from_above = jnp.concatenate([jnp.zeros_like(sinking[:, :, :1]), sinking[:, :, :-1]], axis=2)
    return (values + (flux_west - mass_flux) + diffusion * (east_cells + west_cells - 2.0 * values)
            + lat_terms(values) + (from_above - sinking))


def adjoint_step(values, wind_speed, settling):
    west_cells = jnp.roll(values, 1, 4)
    east_cells = jnp.roll(values, -1, 4)
    from_below = jnp.concatenate([values[:, :, 1:], jnp.zeros_like(values[:, :, :1])], axis=2)
    return (values + wind_speed * (east_cells - values) + diffusion * (east_cells + west_cells - 2.0 * values)
            + lat_terms(values) + settling[None, :, :, None, None] * (from_below - values))


def reference(trajectory, block_weights, wind_speed, settling, source_mask, obs_columns, obs_values, obs_weights):
    highest = lax.Precision.HIGHEST
    fine_cells = trajectory.astype(jnp.float32).reshape(SLOTS, BINS, NLEV, CLAT, BLOCK, CLON, BLOCK)
    coarse = jnp.einsum("sbkiajc,ac->sbkij", fine_cells, block_weights, precision=highest)
    picker = (obs_columns[:, :, None] == jnp.arange(CLON, dtype=jnp.int32)[None, None, :]).astype(jnp.float32)
    control_mask = source_mask.astype(jnp.float32)
    column_scale = 1.0 / (BINS * NLEV)
    correction = jnp.zeros_like(coarse)
    for sweep_index in range(SWEEPS):
        tracer = coarse + correction
        for step_index in range(STEPS):
            tracer = forward_step(tracer, wind_speed, settling)
        columns = jnp.sum(tracer, axis=(1, 2)) * column_scale
        observed = jnp.einsum("sic,ioc->sio", columns, picker, precision=highest)
        misfit = obs_weights * (observed - obs_values)
        spread = jnp.einsum("sio,ioc->sic", misfit, picker, precision=highest) * column_scale
        adjoint = jnp.broadcast_to(spread[:, None, None], coarse.shape)
        for step_index in range(STEPS):
            adjoint = adjoint_step(adjoint, wind_speed, settling)
        gradient = background * correction + adjoint
        correction = control_mask * (correction - step_length * gradient)
    growth = (BLOCK * BLOCK) * block_weights
    increment = jnp.einsum("sbkij,ac->sbkiajc", correction, growth, precision=highest)
    increment = increment.reshape(SLOTS, BINS, NLEV, NLAT, NLON)
    analysis = (trajectory.astype(jnp.float32) + increment).astype(jnp.bfloat16)
    return analysis, correction
```

```python
import jax
import jax.numpy as jnp
from jax import lax
from jax.experimental import pallas as pl
from jax.experimental.pallas import tpu as pltpu
from jax.sharding import PartitionSpec as P

BLOCK = 8
STEPS = 4
SWEEPS = 2
REACH = STEPS * 2 * SWEEPS
LANES = 128
HALF = LANES // 2
EDGE = 8

diffusion = 0.05
background = 0.1
step_length = 4.0
AXES = ("lon", "lat", "lev")


def lane_iota(rows):
    return lax.broadcasted_iota(jnp.int32, (rows, LANES), 1)


def three_parts(values):
    high = values.astype(jnp.bfloat16)
    rest = values - high.astype(jnp.float32)
    middle = rest.astype(jnp.bfloat16)
    low = (rest - middle.astype(jnp.float32)).astype(jnp.bfloat16)
    return jnp.concatenate([high, middle, low], axis=0)


def weight_rows(weights):
    picks = lax.broadcasted_iota(jnp.int32, (BLOCK, LANES), 0) == lane_iota(BLOCK) % BLOCK
    return jnp.dot(
        weights,
        picks.astype(jnp.float32),
        precision=lax.Precision.HIGHEST,
        preferred_element_type=jnp.float32,
    )


def restrict_kernel(slots, bins, rows, cols, trajectory, weights, wind, mask, packed):
    rows_of_weights = weight_rows(weights[...])
    groups = slots * bins
    fine = trajectory[...].astype(jnp.float32).reshape(groups * rows, BLOCK, LANES)
    row_sums = jnp.sum(fine * rows_of_weights[None], axis=1)
    cell = lax.broadcasted_iota(jnp.int32, (LANES, LANES), 0) // BLOCK
    pool = (cell == lane_iota(LANES) % cols).astype(jnp.float32).astype(jnp.bfloat16)
    pooled = jnp.dot(three_parts(row_sums), pool, preferred_element_type=jnp.float32)
    count = groups * rows
    pooled = pooled[:count] + pooled[count : 2 * count] + pooled[2 * count :]
    group = lane_iota(rows) // cols
    filler = jnp.zeros((rows, bins * cols), jnp.float32)
    out = jnp.concatenate(
        [filler, wind[0], filler, mask[...].astype(jnp.float32)], axis=1
    )
    for slot in range(slots):
        for size in range(bins):
            start = (slot * bins + size) * rows
            out = jnp.where(
                group == slot * (bins + 1) + size, pooled[start : start + rows], out
            )
    packed[...] = out


def window_start(lat_count, rows, window):
    lat = lax.axis_index("lat")
    own = jnp.where(lat == 0, 0, jnp.where(lat == lat_count - 1, window - rows, REACH))
    return lat, own


def obs_kernel(lat_count, lon_total, rows, cols, window, columns, values, obs_weights, table):
    lat, own = window_start(lat_count, rows, window)
    first = pl.multiple_of(lat * rows - own, 8)
    span = pl.ds(first, window)
    slots = values.shape[0]
    obs = columns.shape[1]

    def turned(pieces):
        pad = jnp.zeros((HALF - window, obs), pieces[0].dtype)
        laid = []
        for piece in pieces:
            laid += [piece, pad] if window < HALF else [piece]
        return jnp.concatenate(laid, axis=0).T

    place = turned([columns[span, :].astype(jnp.float32)] * slots)
    weight = turned([obs_weights[slot, span, :] for slot in range(slots)])
    product = turned([obs_weights[slot, span, :] * values[slot, span, :] for slot in range(slots)])
    sub = lax.broadcasted_iota(jnp.int32, (HALF, LANES), 0)
    start = lax.axis_index("lon") * cols - cols + lon_total
    here = lax.rem(sub + start, lon_total).astype(jnp.float32)
    sum_weight = jnp.zeros((HALF, LANES), jnp.float32)
    sum_product = jnp.zeros((HALF, LANES), jnp.float32)
    for index in range(obs):
        hit = here == place[index : index + 1]
        sum_weight += jnp.where(hit, weight[index : index + 1], 0.0)
        sum_product += jnp.where(hit, product[index : index + 1], 0.0)
    both = jnp.concatenate([sum_weight, sum_product], axis=0).T
    left, right = both[:window], both[HALF : HALF + window]
    low = lane_iota(window) < HALF
    table[0] = jnp.where(low, left, pltpu.roll(right, HALF, 1))
    table[1] = jnp.where(low, pltpu.roll(left, HALF, 1), right)


def cycle_kernel(
    lat_count,
    slots,
    bins,
    rows,
    cols,
    window,
    own_cells,
    near_cells,
    far_cells,
    table,
    settling,
    weights,
    trajectory,
    analysis,
    correction,
    fine,
    here,
    there,
    coarse,
    change,
    winds,
    laid,
    copied,
):
    fetch = pltpu.make_async_copy(trajectory, fine, copied)
    fetch.start()
    levels = 2
    fields = levels * bins
    lat, own = window_start(lat_count, rows, window)
    level = lax.axis_index("lev")
    lon = lax.axis_index("lon")
    near_is_west = lax.rem(lon + level, 2)
    inner = slice(EDGE, EDGE + window)
    north = slice(EDGE + 1, EDGE + 1 + window)
    south = slice(EDGE - 1, EDGE - 1 + window)
    edge = jnp.zeros((EDGE, LANES), jnp.float32)
    for held in (here, there):
        for field in range(fields):
            held[field, :EDGE] = edge
            held[field, EDGE + window :] = edge

    def lay(place, block, rank):
        laid[place, pl.ds(pl.multiple_of(own, 8), rows)] = block[rank, :rows]
        if lat_count == 2:
            rim = pl.multiple_of(jnp.where(lat == 0, rows, 0), 8)
            laid[place, pl.ds(rim, REACH)] = block[rank, rows:]
        else:
            @pl.when(lat == 0)
            def _():
                laid[place, window - REACH :] = jnp.zeros((REACH, LANES), jnp.float32)

            @pl.when(lat == lat_count - 1)
            def _():
                laid[place, :REACH] = jnp.zeros((REACH, LANES), jnp.float32)

            @pl.when(lat > 0)
            def _():
                laid[place, pl.ds(pl.multiple_of(own - REACH, 8), REACH)] = block[rank, rows : rows + REACH]

            @pl.when(lat < lat_count - 1)
            def _():
                laid[place, pl.ds(pl.multiple_of(own + rows, 8), REACH)] = block[rank, rows + REACH :]

    for rank in range(levels):
        at = (rank + level) % levels
        lay(at * 3 + 2 * (1 - near_is_west), near_cells, rank)
        lay(at * 3 + 1, own_cells, rank)
        lay(at * 3 + 2 * near_is_west, far_cells, levels - 1 - rank)

    lane = lane_iota(window)
    spot = lane % HALF // cols
    low = lane < HALF
    mask = None
    for k in range(levels):
        blocks = [laid[3 * k + place] for place in range(3)]

        def gathered(group):
            out = jnp.zeros((window, LANES), jnp.float32)
            for place in range(3):
                turn = (place - group) * cols % LANES
                moved = pltpu.roll(blocks[place], turn, 1) if turn else blocks[place]
                out = jnp.where(spot == place, moved, out)
            return out

        for size in range(bins):
            cells = gathered(size)
            coarse[k * bins + size] = cells
            change[k * bins + size] = jnp.zeros((window, LANES), jnp.float32)
        sides = jnp.zeros((window, LANES), jnp.float32)
        for place in range(3):
            sides = jnp.where(spot == place, pltpu.roll(blocks[place], (place - 3) * cols % LANES, 1), sides)
        turned = pltpu.roll(sides, HALF, 1)
        wind = jnp.where(low, sides, turned)
        winds[3 * k] = 1.0 - 4.0 * diffusion - wind
        winds[3 * k + 1] = pltpu.roll(wind, 1, 1) + diffusion
        winds[3 * k + 2] = wind + diffusion
        if k == 0:
            mask = jnp.where(low, turned, sides)

    rates = [[settling[size, k] for k in range(levels)] for size in range(bins)]

    def spread_of(held, field, k, backward):
        cells = held[field, inner]
        west, east = pltpu.roll(cells, 1, 1), pltpu.roll(cells, LANES - 1, 1)
        swept, other = (east, west) if backward else (west, east)
        near = diffusion * (held[field, north] + held[field, south] + other)
        return cells, near + winds[3 * k + 1 + backward] * swept + winds[3 * k] * cells

    def step(source, target, backward):
        for k in range(levels):
            for size in range(bins):
                field = k * bins + size
                cells, moved = spread_of(source, field, k, backward)
                moved -= rates[size][k] * cells
                if backward and k + 1 < levels:
                    moved += rates[size][k] * source[field + bins, inner]
                if not backward and k > 0:
                    moved += rates[size][k - 1] * source[field - bins, inner]
                target[field, inner] = moved

    def sweep(index, carry):
        for field in range(fields):
            here[field, inner] = coarse[field] + change[field]
        pair = (here, there)
        for count in range(STEPS - 1):
            step(pair[count % 2], pair[(count + 1) % 2], False)
        held, free = pair[(STEPS - 1) % 2], pair[STEPS % 2]
        total = jnp.zeros((window, LANES), jnp.float32)
        for k in range(levels):
            summed = held[k * bins, inner]
            for size in range(1, bins):
                summed += held[k * bins + size, inner]
            free[k, inner] = summed
            total += spread_of(free, k, k, False)[1]
        for size in range(bins):
            total -= rates[size][levels - 1] * held[(levels - 1) * bins + size, inner]
        scale = 1.0 / fields
        held[0, inner] = table[0] * (total * (scale * scale)) - table[1] * scale
        source, target = held, free
        for k in range(levels):
            cells, moved = spread_of(source, 0, k, True)
            for size in range(bins):
                last = k == levels - 1
                target[k * bins + size, inner] = moved - rates[size][k] * cells if last else moved
        for count in range(STEPS - 1):
            source, target = target, source
            step(source, target, True)
        for field in range(fields):
            old = change[field]
            gradient = background * old + target[field, inner]
            change[field] = mask * (old - step_length * gradient)
        return carry

    lax.fori_loop(0, SWEEPS, sweep, 0)

    at = pl.ds(pl.multiple_of(own, 8), rows)
    final = [change[level * bins + size, at] for size in range(bins)]
    for size in range(bins):
        for slot in range(slots):
            moved = pltpu.roll(final[size], (LANES - slot * HALF - cols) % LANES, 1)
            correction[slot, size, 0] = moved[:, :cols]
    source_lane = lax.broadcasted_iota(jnp.int32, (LANES, slots * LANES), 0)
    target_lane = lax.broadcasted_iota(jnp.int32, (LANES, slots * LANES), 1)
    picks = source_lane == target_lane // LANES * HALF + cols + target_lane % LANES // BLOCK
    picks = picks.astype(jnp.float32).astype(jnp.bfloat16)
    wide = jnp.dot(three_parts(jnp.concatenate(final, axis=0)), picks, preferred_element_type=jnp.float32)
    count = bins * rows
    wide = wide[:count] + wide[count : 2 * count] + wide[2 * count :]
    growth = (BLOCK * BLOCK) * weight_rows(weights[...])
    fetch.wait()
    for slot in range(slots):
        for size in range(bins):
            cells = wide[size * rows : (size + 1) * rows, slot * LANES : (slot + 1) * LANES]
            raised = (cells[:, None, :] * growth[None]).reshape(rows * BLOCK, LANES)
            analysis[slot, size, 0] = (fine[slot, size, 0].astype(jnp.float32) + raised).astype(jnp.bfloat16)


def solution(mesh):
    lon_count, lat_count, lev_count = (mesh.shape[axis] for axis in AXES)

    def place_of(lon, lat, lev):
        return (lon % lon_count * lat_count + lat) * lev_count + lev

    def moved(values, source_of):
        pairs = []
        for lon in range(lon_count):
            for lat in range(lat_count):
                for lev in range(lev_count):
                    source = source_of(lon, lat, lev)
                    if source is not None:
                        pairs.append((place_of(*source), place_of(lon, lat, lev)))
        return lax.ppermute(values, AXES, pairs)

    def per_device(
        trajectory,
        block_weights,
        wind_speed,
        settling,
        source_mask,
        obs_columns,
        obs_values,
        obs_weights,
    ):
        slots, bins, _, fine_rows, fine_cols = trajectory.shape
        rows, cols = fine_rows // BLOCK, fine_cols // BLOCK
        rims = min(lat_count - 1, 2)
        window = rows + rims * REACH
        in_vmem = pl.BlockSpec(memory_space=pltpu.VMEM)
        anywhere = pl.BlockSpec(memory_space=pl.ANY)

        def restrict(*refs):
            restrict_kernel(slots, bins, rows, cols, *refs)

        packed = pl.pallas_call(
            restrict,
            out_shape=jax.ShapeDtypeStruct((rows, LANES), jnp.float32),
            in_specs=[in_vmem] * 4,
            out_specs=in_vmem,
        )(trajectory, block_weights, wind_speed, source_mask)

        def tabulate(*refs):
            obs_kernel(lat_count, lon_count * cols, rows, cols, window, *refs)

        table = pl.pallas_call(
            tabulate,
            out_shape=jax.ShapeDtypeStruct((2, window, LANES), jnp.float32),
            in_specs=[in_vmem] * 3,
            out_specs=in_vmem,
        )(obs_columns, obs_values, obs_weights)

        other = moved(packed, lambda lon, lat, lev: (lon, lat, 1 - lev))
        levels = jnp.stack([packed, other])
        if lat_count == 2:
            rim = lax.dynamic_slice_in_dim(levels, (1 - lax.axis_index("lat")) * (rows - REACH), REACH, 1)
            rim = moved(rim, lambda lon, lat, lev: (lon, 1 - lat, 1 - lev))
            own = jnp.concatenate([levels, rim[::-1]], axis=1)
        else:
            low = moved(
                levels[:, rows - REACH :],
                lambda lon, lat, lev: (lon, lat - 1, 1 - lev) if lat > 0 else None,
            )
            high = moved(
                levels[:, :REACH],
                lambda lon, lat, lev: (lon, lat + 1, 1 - lev) if lat < lat_count - 1 else None,
            )
            own = jnp.concatenate([levels, low[::-1], high[::-1]], axis=1)
        near = moved(own, lambda lon, lat, lev: (lon ^ 1 if lev == 0 else lon + 1 - 2 * ((lon + 1) % 2), lat, lev))
        far = moved(near, lambda lon, lat, lev: (lon, lat, 1 - lev))

        def cycle(*refs):
            cycle_kernel(lat_count, slots, bins, rows, cols, window, *refs)

        fields = 2 * bins
        field_store = pltpu.VMEM((fields, window, LANES), jnp.float32)
        step_store = pltpu.VMEM((fields, window + 2 * EDGE, LANES), jnp.float32)
        return pl.pallas_call(
            cycle,
            out_shape=(
                jax.ShapeDtypeStruct(trajectory.shape, jnp.bfloat16),
                jax.ShapeDtypeStruct((slots, bins, 1, rows, cols), jnp.float32),
            ),
            in_specs=[in_vmem] * 4 + [pl.BlockSpec(memory_space=pltpu.SMEM), in_vmem, anywhere],
            out_specs=(in_vmem, in_vmem),
            scratch_shapes=[
                pltpu.VMEM(trajectory.shape, jnp.bfloat16),
                step_store,
                step_store,
                field_store,
                field_store,
                pltpu.VMEM((6, window, LANES), jnp.float32),
                pltpu.VMEM((6, window, LANES), jnp.float32),
                pltpu.SemaphoreType.DMA,
            ],
        )(own, near, far, table, settling, block_weights, trajectory)

    placed = (
        P("member", None, "lev", "lat", "lon"),
        P(),
        P("lev", "lat", "lon"),
        P(),
        P("lat", "lon"),
        P("member", None),
        P("member", None, None),
        P("member", None, None),
    )
    return jax.shard_map(
        per_device,
        mesh=mesh,
        in_specs=placed,
        out_specs=(P("member", None, "lev", "lat", "lon"), P("member", None, "lev", "lat", "lon")),
        check_vma=False,
    )
```

```python
import jax
import jax.numpy as jnp
from jax import lax
from jax.experimental import pallas as pl
from jax.experimental.pallas import tpu as pltpu
from jax.sharding import PartitionSpec as P

BLOCK = 8
STEPS = 4
SWEEPS = 2
REACH = STEPS * 2 * SWEEPS
LANES = 128
HALF = LANES // 2
EDGE = 8

diffusion = 0.05
background = 0.1
step_length = 4.0
AXES = ("lon", "lat", "lev")


def lane_iota(rows):
    return lax.broadcasted_iota(jnp.int32, (rows, LANES), 1)


def three_parts(values):
    high = values.astype(jnp.bfloat16)
    rest = values - high.astype(jnp.float32)
    middle = rest.astype(jnp.bfloat16)
    low = (rest - middle.astype(jnp.float32)).astype(jnp.bfloat16)
    return jnp.concatenate([high, middle, low], axis=0)


def weight_rows(weights):
    return jnp.concatenate([weights] * (LANES // BLOCK), axis=1)


def fetch_all(sources, held, copied):
    fetches = [
        pltpu.make_async_copy(source, target, copied.at[index])
        for index, (source, target) in enumerate(zip(sources, held))
    ]
    for fetch in fetches:
        fetch.start()
    for fetch in fetches:
        fetch.wait()


def restrict_kernel(lat_count, slots, bins, rows, cols, *refs):
    sources, packed, held, fine, copied = refs[:4], refs[4], refs[5:9], refs[9], refs[10]
    fetch_all(sources, held, copied)
    trajectory, weights, wind, mask = held
    rows_of_weights = weight_rows(weights[...])
    count = slots * bins * rows
    fine[...] = trajectory[...].reshape(count * BLOCK, LANES).astype(jnp.float32)
    row_sums = fine[pl.ds(0, count, stride=BLOCK), :] * rows_of_weights[:1]
    for index in range(1, BLOCK):
        row_sums += fine[pl.ds(index, count, stride=BLOCK), :] * rows_of_weights[index : index + 1]
    cell = lax.broadcasted_iota(jnp.int32, (LANES, LANES), 0) // BLOCK
    pool = (cell == lane_iota(LANES) % cols).astype(jnp.float32).astype(jnp.bfloat16)
    pooled = jnp.dot(three_parts(row_sums), pool, preferred_element_type=jnp.float32)
    pooled = pooled[:count] + pooled[count : 2 * count] + pooled[2 * count :]
    group = lane_iota(rows) // cols
    filler = jnp.zeros((bins * cols, rows), jnp.float32)
    out = jnp.concatenate([filler, wind[0], filler, mask[...].astype(jnp.float32)], axis=0).T
    for slot in range(slots):
        for size in range(bins):
            start = (slot * bins + size) * rows
            out = jnp.where(
                group == slot * (bins + 1) + size, pooled[start : start + rows], out
            )
    if lat_count == 2:
        start = pl.multiple_of(jnp.where(lax.axis_index("lat") == 0, rows - REACH, 0), 8)
        packed[pl.ds(start, REACH)] = out[:REACH]
        packed[pl.ds(pl.multiple_of(rows - REACH - start, 8), REACH)] = out[REACH:]
    else:
        packed[...] = out


def window_start(lat_count, rows, window):
    lat = lax.axis_index("lat")
    own = jnp.where(lat == 0, 0, jnp.where(lat == lat_count - 1, window - rows, REACH))
    return lat, own


def obs_kernel(lat_count, lon_total, rows, cols, window, *refs):
    sources, (table, scales), held, copied = refs[:5], refs[5:7], refs[7:12], refs[12]
    fetch_all(sources, held, copied)
    columns, values, obs_weights, settling, weights = held
    lat, own = window_start(lat_count, rows, window)
    first = lat * rows - own
    slots, obs, lat_total = values.shape
    wide = -(-lat_total // LANES) * LANES
    low = lane_iota(obs) < HALF

    def windowed(array):
        if wide > lat_total:
            array = jnp.concatenate([array, jnp.zeros((obs, wide - lat_total), array.dtype)], axis=1)
        return pltpu.roll(array, lax.rem(wide - first, wide), 1)[:, :LANES]

    def paired(first_slot, second_slot):
        return jnp.where(low, windowed(first_slot), pltpu.roll(windowed(second_slot), HALF, 1))

    held = columns[...].astype(jnp.float32)
    place = paired(held, held)
    weight = paired(obs_weights[0], obs_weights[1])
    product = paired(obs_weights[0] * values[0], obs_weights[1] * values[1])
    sub = lax.broadcasted_iota(jnp.int32, (HALF, LANES), 0)
    start = lax.axis_index("lon") * cols - cols + lon_total
    here = lax.rem(sub + start, lon_total).astype(jnp.float32)
    sum_weight = jnp.zeros((HALF, LANES), jnp.float32)
    sum_product = jnp.zeros((HALF, LANES), jnp.float32)
    for index in range(obs):
        hit = here == place[index : index + 1]
        sum_weight += jnp.where(hit, weight[index : index + 1], 0.0)
        sum_product += jnp.where(hit, product[index : index + 1], 0.0)
    both = jnp.concatenate([sum_weight, sum_product], axis=0).T
    left, right = both[:window], both[HALF : HALF + window]
    low = lane_iota(window) < HALF
    table[0] = jnp.where(low, left, pltpu.roll(right, HALF, 1))
    table[1] = jnp.where(low, pltpu.roll(left, HALF, 1), right)
    levels, bins = settling.shape
    for k in range(levels):
        for size in range(bins):
            rate = settling[k : k + 1, size : size + 1]
            scales[k * bins + size] = jnp.broadcast_to(rate, (BLOCK, LANES))
    scales[levels * bins] = (BLOCK * BLOCK) * weight_rows(weights[...])


def cycle_kernel(
    lat_count,
    slots,
    bins,
    rows,
    cols,
    window,
    own_cells,
    near_cells,
    far_cells,
    table,
    scales,
    trajectory,
    analysis,
    correction,
    fine,
    here,
    there,
    coarse,
    change,
    winds,
    laid,
    copied,
):
    fetch = pltpu.make_async_copy(trajectory, fine, copied)
    fetch.start()
    levels = 2
    fields = levels * bins
    lat, own = window_start(lat_count, rows, window)
    level = lax.axis_index("lev")
    lon = lax.axis_index("lon")
    near_is_west = lax.rem(lon + level, 2)
    inner = slice(EDGE, EDGE + window)
    north = slice(EDGE + 1, EDGE + 1 + window)
    south = slice(EDGE - 1, EDGE - 1 + window)
    edge = jnp.zeros((EDGE, LANES), jnp.float32)
    for held in (here, there):
        for field in range(fields):
            held[field, :EDGE] = edge
            held[field, EDGE + window :] = edge

    def lay(place, block, rank):
        if lat_count == 2:
            outer = pl.multiple_of(lat * 2 * REACH, 8)
            laid[place, REACH : 2 * REACH] = block[rank, :REACH]
            laid[place, pl.ds(outer, REACH)] = block[rank, REACH:rows]
            laid[place, pl.ds(pl.multiple_of(2 * REACH - outer, 8), REACH)] = block[rank, rows:]
        else:
            laid[place, pl.ds(pl.multiple_of(own, 8), rows)] = block[rank, :rows]

            @pl.when(lat == 0)
            def _():
                laid[place, window - REACH :] = jnp.zeros((REACH, LANES), jnp.float32)

            @pl.when(lat == lat_count - 1)
            def _():
                laid[place, :REACH] = jnp.zeros((REACH, LANES), jnp.float32)

            @pl.when(lat > 0)
            def _():
                laid[place, pl.ds(pl.multiple_of(own - REACH, 8), REACH)] = block[rank, rows : rows + REACH]

            @pl.when(lat < lat_count - 1)
            def _():
                laid[place, pl.ds(pl.multiple_of(own + rows, 8), REACH)] = block[rank, rows + REACH :]

    for rank in range(levels):
        at = (rank + level) % levels
        lay(at * 3 + 2 * (1 - near_is_west), near_cells, rank)
        lay(at * 3 + 1, own_cells, rank)
        lay(at * 3 + 2 * near_is_west, far_cells, levels - 1 - rank)

    lane = lane_iota(window)
    spot = lane % HALF // cols
    low = lane < HALF
    mask = None
    for k in range(levels):
        blocks = [laid[3 * k + place] for place in range(3)]

        def gathered(group):
            out = jnp.zeros((window, LANES), jnp.float32)
            for place in range(3):
                turn = (place - group) * cols % LANES
                moved = pltpu.roll(blocks[place], turn, 1) if turn else blocks[place]
                out = jnp.where(spot == place, moved, out)
            return out

        for size in range(bins):
            cells = gathered(size)
            coarse[k * bins + size] = cells
            change[k * bins + size] = jnp.zeros((window, LANES), jnp.float32)
        sides = jnp.zeros((window, LANES), jnp.float32)
        for place in range(3):
            sides = jnp.where(spot == place, pltpu.roll(blocks[place], (place - 3) * cols % LANES, 1), sides)
        turned = pltpu.roll(sides, HALF, 1)
        wind = jnp.where(low, sides, turned)
        winds[3 * k] = 1.0 - 4.0 * diffusion - wind
        winds[3 * k + 1] = pltpu.roll(wind, 1, 1) + diffusion
        winds[3 * k + 2] = wind + diffusion
        if k == 0:
            mask = jnp.where(low, turned, sides)

    rates = [[scales[k * bins + size, :1] for k in range(levels)] for size in range(bins)]

    def spread_of(held, field, k, backward):
        cells = held[field, inner]
        west, east = pltpu.roll(cells, 1, 1), pltpu.roll(cells, LANES - 1, 1)
        swept, other = (east, west) if backward else (west, east)
        near = diffusion * (held[field, north] + held[field, south] + other)
        return cells, near + winds[3 * k + 1 + backward] * swept + winds[3 * k] * cells

    def step(source, target, backward):
        for k in range(levels):
            for size in range(bins):
                field = k * bins + size
                cells, moved = spread_of(source, field, k, backward)
                moved -= rates[size][k] * cells
                if backward and k + 1 < levels:
                    moved += rates[size][k] * source[field + bins, inner]
                if not backward and k > 0:
                    moved += rates[size][k - 1] * source[field - bins, inner]
                target[field, inner] = moved

    def sweep(index, carry):
        for field in range(fields):
            here[field, inner] = coarse[field] + change[field]
        pair = (here, there)
        for count in range(STEPS - 1):
            step(pair[count % 2], pair[(count + 1) % 2], False)
        held, free = pair[(STEPS - 1) % 2], pair[STEPS % 2]
        total = jnp.zeros((window, LANES), jnp.float32)
        for k in range(levels):
            summed = held[k * bins, inner]
            for size in range(1, bins):
                summed += held[k * bins + size, inner]
            free[k, inner] = summed
            total += spread_of(free, k, k, False)[1]
        for size in range(bins):
            total -= rates[size][levels - 1] * held[(levels - 1) * bins + size, inner]
        scale = 1.0 / fields
        held[0, inner] = table[0] * (total * (scale * scale)) - table[1] * scale
        source, target = held, free
        for k in range(levels):
            cells, moved = spread_of(source, 0, k, True)
            for size in range(bins):
                last = k == levels - 1
                target[k * bins + size, inner] = moved - rates[size][k] * cells if last else moved
        for count in range(STEPS - 1):
            source, target = target, source
            step(source, target, True)
        for field in range(fields):
            old = change[field]
            gradient = background * old + target[field, inner]
            change[field] = mask * (old - step_length * gradient)
        return carry

    lax.fori_loop(0, SWEEPS, sweep, 0)

    at = pl.ds(pl.multiple_of(own, 8), rows)
    final = [change[level * bins + size, at] for size in range(bins)]
    for size in range(bins):
        turned = final[size].T
        for slot in range(slots):
            start = slot * HALF + cols
            correction[slot, size, 0] = turned[start : start + cols]
    source_lane = lax.broadcasted_iota(jnp.int32, (LANES, slots * LANES), 0)
    target_lane = lax.broadcasted_iota(jnp.int32, (LANES, slots * LANES), 1)
    picks = source_lane == target_lane // LANES * HALF + cols + target_lane % LANES // BLOCK
    picks = picks.astype(jnp.float32).astype(jnp.bfloat16)
    wide = jnp.dot(three_parts(jnp.concatenate(final, axis=0)), picks, preferred_element_type=jnp.float32)
    count = bins * rows
    wide = wide[:count] + wide[count : 2 * count] + wide[2 * count :]
    growth = scales[levels * bins]
    fetch.wait()
    for slot in range(slots):
        for size in range(bins):
            cells = wide[size * rows : (size + 1) * rows, slot * LANES : (slot + 1) * LANES]
            raised = (cells[:, None, :] * growth[None]).reshape(rows * BLOCK, LANES)
            analysis[slot, size, 0] = (fine[slot, size, 0].astype(jnp.float32) + raised).astype(jnp.bfloat16)


def solution(mesh):
    lon_count, lat_count, lev_count = (mesh.shape[axis] for axis in AXES)

    def place_of(lon, lat, lev):
        return (lon % lon_count * lat_count + lat) * lev_count + lev

    def moved(values, source_of):
        pairs = []
        for lon in range(lon_count):
            for lat in range(lat_count):
                for lev in range(lev_count):
                    source = source_of(lon, lat, lev)
                    if source is not None:
                        pairs.append((place_of(*source), place_of(lon, lat, lev)))
        return lax.ppermute(values, AXES, pairs)

    def per_device(
        trajectory,
        block_weights,
        wind_speed,
        settling,
        source_mask,
        obs_columns,
        obs_values,
        obs_weights,
    ):
        slots, bins, _, fine_rows, fine_cols = trajectory.shape
        rows, cols = fine_rows // BLOCK, fine_cols // BLOCK
        rims = min(lat_count - 1, 2)
        window = rows + rims * REACH
        small = pltpu.CompilerParams(vmem_limit_bytes=8 * 1024 * 1024)
        in_vmem = pl.BlockSpec(memory_space=pltpu.VMEM)

        def kept(array):
            return pltpu.with_memory_space_constraint(array, pltpu.HBM)

        in_hbm = pl.BlockSpec(memory_space=pltpu.HBM)

        def restrict(*refs):
            restrict_kernel(lat_count, slots, bins, rows, cols, *refs)

        packed = pl.pallas_call(
            restrict,
            out_shape=pltpu.VMEM((rows, LANES), jnp.float32),
            in_specs=[in_hbm] * 4,
            out_specs=in_vmem,
            scratch_shapes=[
                pltpu.VMEM(trajectory.shape, jnp.bfloat16),
                pltpu.VMEM((BLOCK, BLOCK), jnp.float32),
                pltpu.VMEM((1, cols, rows), jnp.float32),
                pltpu.VMEM((cols, rows), jnp.int32),
                pltpu.VMEM((slots * bins * fine_rows, LANES), jnp.float32),
                pltpu.SemaphoreType.DMA((4,)),
            ],
            compiler_params=small,
        )(*map(kept, (trajectory, block_weights, wind_speed.swapaxes(1, 2), source_mask.T)))

        def tabulate(*refs):
            obs_kernel(lat_count, lon_count * cols, rows, cols, window, *refs)

        observed = (
            obs_columns.T,
            obs_values.swapaxes(1, 2),
            obs_weights.swapaxes(1, 2),
            settling.T,
            block_weights,
        )
        table, scales = pl.pallas_call(
            tabulate,
            out_shape=(
                pltpu.VMEM((2, window, LANES), jnp.float32),
                pltpu.VMEM((2 * bins + 1, BLOCK, LANES), jnp.float32),
            ),
            in_specs=[in_hbm] * 5,
            out_specs=(in_vmem, in_vmem),
            scratch_shapes=[pltpu.VMEM(array.shape, array.dtype) for array in observed]
            + [pltpu.SemaphoreType.DMA((5,))],
            compiler_params=small,
        )(*map(kept, observed))

        other = moved(packed, lambda lon, lat, lev: (lon, lat, 1 - lev))
        levels = jnp.stack([packed, other])
        if lat_count == 2:
            rim = moved(levels[:, :REACH], lambda lon, lat, lev: (lon, 1 - lat, 1 - lev))
            own = jnp.concatenate([levels, rim[::-1]], axis=1)
        else:
            low = moved(
                levels[:, rows - REACH :],
                lambda lon, lat, lev: (lon, lat - 1, 1 - lev) if lat > 0 else None,
            )
            high = moved(
                levels[:, :REACH],
                lambda lon, lat, lev: (lon, lat + 1, 1 - lev) if lat < lat_count - 1 else None,
            )
            own = jnp.concatenate([levels, low[::-1], high[::-1]], axis=1)
        near = moved(own, lambda lon, lat, lev: (lon ^ 1 if lev == 0 else lon + 1 - 2 * ((lon + 1) % 2), lat, lev))
        near, table, scales = lax.optimization_barrier((near, table, scales))
        far = moved(near, lambda lon, lat, lev: (lon, lat, 1 - lev))

        def cycle(*refs):
            cycle_kernel(lat_count, slots, bins, rows, cols, window, *refs)

        fields = 2 * bins
        field_store = pltpu.VMEM((fields, window, LANES), jnp.float32)
        step_store = pltpu.VMEM((fields, window + 2 * EDGE, LANES), jnp.float32)
        analysis, correction = pl.pallas_call(
            cycle,
            out_shape=(
                jax.ShapeDtypeStruct(trajectory.shape, jnp.bfloat16),
                jax.ShapeDtypeStruct((slots, bins, 1, cols, rows), jnp.float32),
            ),
            in_specs=[in_vmem] * 5 + [in_hbm],
            out_specs=(in_vmem, in_vmem),
            scratch_shapes=[
                pltpu.VMEM(trajectory.shape, jnp.bfloat16),
                step_store,
                step_store,
                field_store,
                field_store,
                pltpu.VMEM((6, window, LANES), jnp.float32),
                pltpu.VMEM((6, window, LANES), jnp.float32),
                pltpu.SemaphoreType.DMA,
            ],
            compiler_params=small,
        )(own, near, far, table, scales, trajectory)
        return analysis, correction.swapaxes(3, 4)

    placed = (
        P("member", None, "lev", "lat", "lon"),
        P(),
        P("lev", "lat", "lon"),
        P(),
        P("lat", "lon"),
        P("member", None),
        P("member", None, None),
        P("member", None, None),
    )
    return jax.shard_map(
        per_device,
        mesh=mesh,
        in_specs=placed,
        out_specs=(P("member", None, "lev", "lat", "lon"), P("member", None, "lev", "lat", "lon")),
        check_vma=False,
    )
```

```python
import jax
import jax.numpy as jnp
from jax import lax
from jax.experimental import pallas as pl
from jax.experimental.pallas import tpu as pltpu
from jax.sharding import PartitionSpec as P

BLOCK = 8
STEPS = 4
SWEEPS = 2
REACH = STEPS * 2 * SWEEPS
LANES = 128
HALF = LANES // 2
EDGE = 8

diffusion = 0.05
background = 0.1
step_length = 4.0
AXES = ("lon", "lat", "lev")


def lane_iota(rows):
    return lax.broadcasted_iota(jnp.int32, (rows, LANES), 1)


def three_parts(values):
    high = values.astype(jnp.bfloat16)
    rest = values - high.astype(jnp.float32)
    middle = rest.astype(jnp.bfloat16)
    low = (rest - middle.astype(jnp.float32)).astype(jnp.bfloat16)
    return jnp.concatenate([high, middle, low], axis=0)


def weight_rows(weights):
    return jnp.concatenate([weights] * (LANES // BLOCK), axis=1)


def fetch_all(sources, held, copied):
    fetches = [
        pltpu.make_async_copy(source, target, copied.at[index])
        for index, (source, target) in enumerate(zip(sources, held))
    ]
    for fetch in fetches:
        fetch.start()
    for fetch in fetches:
        fetch.wait()


def restrict_kernel(lat_count, slots, bins, rows, cols, *refs):
    sources, packed, held, fine, copied = refs[:4], refs[4], refs[5:9], refs[9], refs[10]
    fetch_all(sources, held, copied)
    trajectory, weights, wind, mask = held
    rows_of_weights = weight_rows(weights[...])
    count = slots * bins * rows
    fine[...] = trajectory[...].reshape(count * BLOCK, LANES).astype(jnp.float32)
    row_sums = fine[pl.ds(0, count, stride=BLOCK), :] * rows_of_weights[:1]
    for index in range(1, BLOCK):
        row_sums += fine[pl.ds(index, count, stride=BLOCK), :] * rows_of_weights[index : index + 1]
    cell = lax.broadcasted_iota(jnp.int32, (LANES, LANES), 0) // BLOCK
    pool = (cell == lane_iota(LANES) % cols).astype(jnp.float32).astype(jnp.bfloat16)
    pooled = jnp.dot(three_parts(row_sums), pool, preferred_element_type=jnp.float32)
    pooled = pooled[:count] + pooled[count : 2 * count] + pooled[2 * count :]
    group = lane_iota(rows) // cols
    filler = jnp.zeros((bins * cols, rows), jnp.float32)
    out = jnp.concatenate([filler, wind[0], filler, mask[...].astype(jnp.float32)], axis=0).T
    for slot in range(slots):
        for size in range(bins):
            start = (slot * bins + size) * rows
            out = jnp.where(
                group == slot * (bins + 1) + size, pooled[start : start + rows], out
            )
    if lat_count == 2:
        start = pl.multiple_of(jnp.where(lax.axis_index("lat") == 0, rows - REACH, 0), 8)
        packed[pl.ds(start, REACH)] = out[:REACH]
        packed[pl.ds(pl.multiple_of(rows - REACH - start, 8), REACH)] = out[REACH:]
    else:
        packed[...] = out


def window_start(lat_count, rows, window):
    lat = lax.axis_index("lat")
    own = jnp.where(lat == 0, 0, jnp.where(lat == lat_count - 1, window - rows, REACH))
    return lat, own


def obs_kernel(lat_count, lon_total, rows, cols, window, *refs):
    sources, (table, scales), held, copied = refs[:5], refs[5:7], refs[7:12], refs[12]
    fetch_all(sources, held, copied)
    columns, values, obs_weights, settling, weights = held
    lat, own = window_start(lat_count, rows, window)
    first = lat * rows - own
    slots, obs, lat_total = values.shape
    wide = -(-lat_total // LANES) * LANES
    low = lane_iota(obs) < HALF

    def windowed(array):
        if wide > lat_total:
            array = jnp.concatenate([array, jnp.zeros((obs, wide - lat_total), array.dtype)], axis=1)
        return pltpu.roll(array, lax.rem(wide - first, wide), 1)[:, :LANES]

    def paired(first_slot, second_slot):
        return jnp.where(low, windowed(first_slot), pltpu.roll(windowed(second_slot), HALF, 1))

    held = columns[...].astype(jnp.float32)
    place = paired(held, held)
    weight = paired(obs_weights[0], obs_weights[1])
    product = paired(obs_weights[0] * values[0], obs_weights[1] * values[1])
    sub = lax.broadcasted_iota(jnp.int32, (HALF, LANES), 0)
    start = lax.axis_index("lon") * cols - cols + lon_total
    here = lax.rem(sub + start, lon_total).astype(jnp.float32)
    sum_weight = jnp.zeros((HALF, LANES), jnp.float32)
    sum_product = jnp.zeros((HALF, LANES), jnp.float32)
    for index in range(obs):
        hit = here == place[index : index + 1]
        sum_weight += jnp.where(hit, weight[index : index + 1], 0.0)
        sum_product += jnp.where(hit, product[index : index + 1], 0.0)
    both = jnp.concatenate([sum_weight, sum_product], axis=0).T
    left, right = both[:window], both[HALF : HALF + window]
    low = lane_iota(window) < HALF
    table[0] = jnp.where(low, left, pltpu.roll(right, HALF, 1))
    table[1] = jnp.where(low, pltpu.roll(left, HALF, 1), right)
    levels, bins = settling.shape
    for k in range(levels):
        for size in range(bins):
            rate = settling[k : k + 1, size : size + 1]
            scales[k * bins + size] = jnp.broadcast_to(rate, (BLOCK, LANES))
    scales[levels * bins] = (BLOCK * BLOCK) * weight_rows(weights[...])


def cycle_kernel(
    lat_count,
    slots,
    bins,
    rows,
    cols,
    window,
    own_cells,
    near_cells,
    near_rims,
    far,
    table,
    scales,
    trajectory,
    analysis,
    correction,
    fine,
    here,
    there,
    coarse,
    change,
    winds,
    laid,
    copied,
):
    fetch = pltpu.make_async_copy(trajectory, fine, copied)
    fetch.start()
    levels = 2
    fields = levels * bins
    lat, own = window_start(lat_count, rows, window)
    level = lax.axis_index("lev")
    lon = lax.axis_index("lon")
    near_is_west = lax.rem(lon + level, 2)
    inner = slice(EDGE, EDGE + window)
    north = slice(EDGE + 1, EDGE + 1 + window)
    south = slice(EDGE - 1, EDGE - 1 + window)
    edge = jnp.zeros((EDGE, LANES), jnp.float32)
    for held in (here, there):
        for field in range(fields):
            held[field, :EDGE] = edge
            held[field, EDGE + window :] = edge

    def lay(place, block, rims):
        if lat_count == 2:
            outer = pl.multiple_of(lat * 2 * REACH, 8)
            laid[place, REACH : 2 * REACH] = block[:REACH]
            laid[place, pl.ds(outer, REACH)] = block[REACH:]
            laid[place, pl.ds(pl.multiple_of(2 * REACH - outer, 8), REACH)] = rims[...]
        else:
            laid[place, pl.ds(pl.multiple_of(own, 8), rows)] = block[...]

            @pl.when(lat == 0)
            def _():
                laid[place, window - REACH :] = jnp.zeros((REACH, LANES), jnp.float32)

            @pl.when(lat == lat_count - 1)
            def _():
                laid[place, :REACH] = jnp.zeros((REACH, LANES), jnp.float32)

            @pl.when(lat > 0)
            def _():
                laid[place, pl.ds(pl.multiple_of(own - REACH, 8), REACH)] = rims[:REACH]

            @pl.when(lat < lat_count - 1)
            def _():
                laid[place, pl.ds(pl.multiple_of(own + rows, 8), REACH)] = rims[REACH:]

    height = window - rows

    def far_cells(rank):
        return far.at[pl.ds(rank * rows, rows)]

    def far_rims(rank):
        return far.at[pl.ds(levels * rows + rank * height, height)]

    for rank in range(levels):
        at = (rank + level) % levels
        lay(at * 3 + 1, own_cells.at[rank], far_rims(0) if rank else near_rims.at[0])
        lay(at * 3 + 2 * (1 - near_is_west), near_cells.at[rank], near_rims.at[1 + rank])
        lay(at * 3 + 2 * near_is_west, far_cells(1 - rank), far_rims(2 - rank))

    lane = lane_iota(window)
    spot = lane % HALF // cols
    low = lane < HALF
    mask = None
    for k in range(levels):
        blocks = [laid[3 * k + place] for place in range(3)]

        def gathered(group):
            out = jnp.zeros((window, LANES), jnp.float32)
            for place in range(3):
                turn = (place - group) * cols % LANES
                moved = pltpu.roll(blocks[place], turn, 1) if turn else blocks[place]
                out = jnp.where(spot == place, moved, out)
            return out

        for size in range(bins):
            cells = gathered(size)
            coarse[k * bins + size] = cells
            change[k * bins + size] = jnp.zeros((window, LANES), jnp.float32)
        sides = jnp.zeros((window, LANES), jnp.float32)
        for place in range(3):
            sides = jnp.where(spot == place, pltpu.roll(blocks[place], (place - 3) * cols % LANES, 1), sides)
        turned = pltpu.roll(sides, HALF, 1)
        wind = jnp.where(low, sides, turned)
        winds[3 * k] = 1.0 - 4.0 * diffusion - wind
        winds[3 * k + 1] = pltpu.roll(wind, 1, 1) + diffusion
        winds[3 * k + 2] = wind + diffusion
        if k == 0:
            mask = jnp.where(low, turned, sides)

    rates = [[scales[k * bins + size, :1] for k in range(levels)] for size in range(bins)]

    def spread_of(held, field, k, backward):
        cells = held[field, inner]
        west, east = pltpu.roll(cells, 1, 1), pltpu.roll(cells, LANES - 1, 1)
        swept, other = (east, west) if backward else (west, east)
        near = diffusion * (held[field, north] + held[field, south] + other)
        return cells, near + winds[3 * k + 1 + backward] * swept + winds[3 * k] * cells

    def step(source, target, backward):
        for k in range(levels):
            for size in range(bins):
                field = k * bins + size
                cells, moved = spread_of(source, field, k, backward)
                moved -= rates[size][k] * cells
                if backward and k + 1 < levels:
                    moved += rates[size][k] * source[field + bins, inner]
                if not backward and k > 0:
                    moved += rates[size][k - 1] * source[field - bins, inner]
                target[field, inner] = moved

    def sweep(index, carry):
        for field in range(fields):
            here[field, inner] = coarse[field] + change[field]
        pair = (here, there)
        for count in range(STEPS - 1):
            step(pair[count % 2], pair[(count + 1) % 2], False)
        held, free = pair[(STEPS - 1) % 2], pair[STEPS % 2]
        total = jnp.zeros((window, LANES), jnp.float32)
        for k in range(levels):
            summed = held[k * bins, inner]
            for size in range(1, bins):
                summed += held[k * bins + size, inner]
            free[k, inner] = summed
            total += spread_of(free, k, k, False)[1]
        for size in range(bins):
            total -= rates[size][levels - 1] * held[(levels - 1) * bins + size, inner]
        scale = 1.0 / fields
        held[0, inner] = table[0] * (total * (scale * scale)) - table[1] * scale
        source, target = held, free
        for k in range(levels):
            cells, moved = spread_of(source, 0, k, True)
            for size in range(bins):
                last = k == levels - 1
                target[k * bins + size, inner] = moved - rates[size][k] * cells if last else moved
        for count in range(STEPS - 1):
            source, target = target, source
            step(source, target, True)
        for field in range(fields):
            old = change[field]
            gradient = background * old + target[field, inner]
            change[field] = mask * (old - step_length * gradient)
        return carry

    lax.fori_loop(0, SWEEPS, sweep, 0)

    at = pl.ds(pl.multiple_of(own, 8), rows)
    final = [change[level * bins + size, at] for size in range(bins)]
    for size in range(bins):
        turned = final[size].T
        for slot in range(slots):
            start = slot * HALF + cols
            correction[slot, size, 0] = turned[start : start + cols]
    source_lane = lax.broadcasted_iota(jnp.int32, (LANES, slots * LANES), 0)
    target_lane = lax.broadcasted_iota(jnp.int32, (LANES, slots * LANES), 1)
    picks = source_lane == target_lane // LANES * HALF + cols + target_lane % LANES // BLOCK
    picks = picks.astype(jnp.float32).astype(jnp.bfloat16)
    wide = jnp.dot(three_parts(jnp.concatenate(final, axis=0)), picks, preferred_element_type=jnp.float32)
    count = bins * rows
    wide = wide[:count] + wide[count : 2 * count] + wide[2 * count :]
    growth = scales[levels * bins]
    fetch.wait()
    for slot in range(slots):
        for size in range(bins):
            cells = wide[size * rows : (size + 1) * rows, slot * LANES : (slot + 1) * LANES]
            raised = (cells[:, None, :] * growth[None]).reshape(rows * BLOCK, LANES)
            analysis[slot, size, 0] = (fine[slot, size, 0].astype(jnp.float32) + raised).astype(jnp.bfloat16)


def solution(mesh):
    lon_count, lat_count, lev_count = (mesh.shape[axis] for axis in AXES)

    def place_of(lon, lat, lev):
        return (lon % lon_count * lat_count + lat) * lev_count + lev

    def moved(values, source_of):
        pairs = []
        for lon in range(lon_count):
            for lat in range(lat_count):
                for lev in range(lev_count):
                    source = source_of(lon, lat, lev)
                    if source is not None:
                        pairs.append((place_of(*source), place_of(lon, lat, lev)))
        return lax.ppermute(values, AXES, pairs)

    def per_device(
        trajectory,
        block_weights,
        wind_speed,
        settling,
        source_mask,
        obs_columns,
        obs_values,
        obs_weights,
    ):
        slots, bins, _, fine_rows, fine_cols = trajectory.shape
        rows, cols = fine_rows // BLOCK, fine_cols // BLOCK
        rims = min(lat_count - 1, 2)
        window = rows + rims * REACH
        small = pltpu.CompilerParams(vmem_limit_bytes=8 * 1024 * 1024)
        in_vmem = pl.BlockSpec(memory_space=pltpu.VMEM)

        def kept(array):
            return pltpu.with_memory_space_constraint(array, pltpu.HBM)

        in_hbm = pl.BlockSpec(memory_space=pltpu.HBM)

        def restrict(*refs):
            restrict_kernel(lat_count, slots, bins, rows, cols, *refs)

        packed = pl.pallas_call(
            restrict,
            out_shape=pltpu.VMEM((rows, LANES), jnp.float32),
            in_specs=[in_hbm] * 4,
            out_specs=in_vmem,
            scratch_shapes=[
                pltpu.VMEM(trajectory.shape, jnp.bfloat16),
                pltpu.VMEM((BLOCK, BLOCK), jnp.float32),
                pltpu.VMEM((1, cols, rows), jnp.float32),
                pltpu.VMEM((cols, rows), jnp.int32),
                pltpu.VMEM((slots * bins * fine_rows, LANES), jnp.float32),
                pltpu.SemaphoreType.DMA((4,)),
            ],
            compiler_params=small,
        )(*map(kept, (trajectory, block_weights, wind_speed.swapaxes(1, 2), source_mask.T)))

        def tabulate(*refs):
            obs_kernel(lat_count, lon_count * cols, rows, cols, window, *refs)

        observed = (
            obs_columns.T,
            obs_values.swapaxes(1, 2),
            obs_weights.swapaxes(1, 2),
            settling.T,
            block_weights,
        )
        table, scales = pl.pallas_call(
            tabulate,
            out_shape=(
                pltpu.VMEM((2, window, LANES), jnp.float32),
                pltpu.VMEM((2 * bins + 1, BLOCK, LANES), jnp.float32),
            ),
            in_specs=[in_hbm] * 5,
            out_specs=(in_vmem, in_vmem),
            scratch_shapes=[pltpu.VMEM(array.shape, array.dtype) for array in observed]
            + [pltpu.SemaphoreType.DMA((5,))],
            compiler_params=small,
        )(*map(kept, observed))

        own = jnp.stack([packed, moved(packed, lambda lon, lat, lev: (lon, lat, 1 - lev))])
        near = moved(own, lambda lon, lat, lev: (lon ^ 1 if lev == 0 else lon + 1 - 2 * ((lon + 1) % 2), lat, lev))
        near, table, scales = lax.optimization_barrier((near, table, scales))
        held = jnp.concatenate([packed[None], near])
        if lat_count == 2:
            rims = moved(held[:, :REACH], lambda lon, lat, lev: (lon, 1 - lat, lev))
        else:
            low = moved(
                held[:, rows - REACH :], lambda lon, lat, lev: (lon, lat - 1, lev) if lat > 0 else None
            )
            high = moved(
                held[:, :REACH], lambda lon, lat, lev: (lon, lat + 1, lev) if lat < lat_count - 1 else None
            )
            rims = jnp.concatenate([low, high], axis=1)
        brought = jnp.concatenate([near.reshape(-1, LANES), rims.reshape(-1, LANES)])
        far = moved(brought, lambda lon, lat, lev: (lon, lat, 1 - lev))

        def cycle(*refs):
            cycle_kernel(lat_count, slots, bins, rows, cols, window, *refs)

        fields = 2 * bins
        field_store = pltpu.VMEM((fields, window, LANES), jnp.float32)
        step_store = pltpu.VMEM((fields, window + 2 * EDGE, LANES), jnp.float32)
        analysis, correction = pl.pallas_call(
            cycle,
            out_shape=(
                jax.ShapeDtypeStruct(trajectory.shape, jnp.bfloat16),
                jax.ShapeDtypeStruct((slots, bins, 1, cols, rows), jnp.float32),
            ),
            in_specs=[in_vmem] * 6 + [in_hbm],
            out_specs=(in_vmem, in_vmem),
            scratch_shapes=[
                pltpu.VMEM(trajectory.shape, jnp.bfloat16),
                step_store,
                step_store,
                field_store,
                field_store,
                pltpu.VMEM((6, window, LANES), jnp.float32),
                pltpu.VMEM((6, window, LANES), jnp.float32),
                pltpu.SemaphoreType.DMA,
            ],
            compiler_params=small,
        )(own, near, rims, far, table, scales, kept(trajectory))
        return analysis, correction.swapaxes(3, 4)

    placed = (
        P("member", None, "lev", "lat", "lon"),
        P(),
        P("lev", "lat", "lon"),
        P(),
        P("lat", "lon"),
        P("member", None),
        P("member", None, None),
        P("member", None, None),
    )
    return jax.shard_map(
        per_device,
        mesh=mesh,
        in_specs=placed,
        out_specs=(P("member", None, "lev", "lat", "lon"), P("member", None, "lev", "lat", "lon")),
        check_vma=False,
    )
```

```python
import jax
import jax.numpy as jnp
from jax import lax
from jax.experimental import pallas as pl
from jax.experimental.pallas import tpu as pltpu
from jax.sharding import PartitionSpec as P

BLOCK = 8
STEPS = 4
SWEEPS = 2
REACH = STEPS * 2 * SWEEPS
LANES = 128
HALF = LANES // 2
EDGE = 8

diffusion = 0.05
background = 0.1
step_length = 4.0
AXES = ("lon", "lat", "lev")


def lane_iota(rows):
    return lax.broadcasted_iota(jnp.int32, (rows, LANES), 1)


def three_parts(values):
    high = values.astype(jnp.bfloat16)
    rest = values - high.astype(jnp.float32)
    middle = rest.astype(jnp.bfloat16)
    low = (rest - middle.astype(jnp.float32)).astype(jnp.bfloat16)
    return jnp.concatenate([high, middle, low], axis=1)


def weight_rows(weights):
    return jnp.concatenate([weights] * (LANES // BLOCK), axis=1)


def fetches_of(sources, held, copied):
    return [
        pltpu.make_async_copy(source, target, copied.at[index])
        for index, (source, target) in enumerate(zip(sources, held))
    ]


def restrict_kernel(lat_count, slots, bins, rows, cols, *refs):
    sources, packed, held, fine, copied = refs[:4], refs[4], refs[5:9], refs[9], refs[10]
    trajectory, weights, wind, mask = held
    parts = [(slot, size) for slot in range(slots) for size in range(bins)]
    fetches = fetches_of(
        [*sources[1:], *(sources[0].at[at] for at in parts)],
        [*held[1:], *(trajectory.at[at] for at in parts)],
        copied,
    )
    for fetch in fetches:
        fetch.start()
    for fetch in fetches[:3]:
        fetch.wait()
    rows_of_weights = weight_rows(weights[...])
    row_sums = []
    for index, at in enumerate(parts):
        fetches[3 + index].wait()
        start = index * rows * BLOCK
        fine[start : start + rows * BLOCK] = trajectory[at].reshape(rows * BLOCK, LANES).astype(jnp.float32)
        total = fine[pl.ds(start, rows, stride=BLOCK), :] * rows_of_weights[:1]
        for row in range(1, BLOCK):
            total += fine[pl.ds(start + row, rows, stride=BLOCK), :] * rows_of_weights[row : row + 1]
        row_sums.append(total)
    row_sums = jnp.concatenate(row_sums)
    cell = lax.broadcasted_iota(jnp.int32, (LANES, LANES), 0) // BLOCK
    pool = (cell == lane_iota(LANES) % cols).astype(jnp.float32).astype(jnp.bfloat16)
    pooled = jnp.dot(three_parts(row_sums), jnp.concatenate([pool] * 3), preferred_element_type=jnp.float32)
    group = lane_iota(rows) // cols
    filler = jnp.zeros((bins * cols, rows), jnp.float32)
    out = jnp.concatenate([filler, wind[0], filler, mask[...].astype(jnp.float32)], axis=0).T
    for slot in range(slots):
        for size in range(bins):
            start = (slot * bins + size) * rows
            out = jnp.where(
                group == slot * (bins + 1) + size, pooled[start : start + rows], out
            )
    if lat_count == 2:
        start = pl.multiple_of(jnp.where(lax.axis_index("lat") == 0, rows - REACH, 0), 8)
        packed[pl.ds(start, REACH)] = out[:REACH]
        packed[pl.ds(pl.multiple_of(rows - REACH - start, 8), REACH)] = out[REACH:]
    else:
        packed[...] = out


def window_start(lat_count, rows, window):
    lat = lax.axis_index("lat")
    own = jnp.where(lat == 0, 0, jnp.where(lat == lat_count - 1, window - rows, REACH))
    return lat, own


def obs_kernel(lat_count, lon_total, rows, cols, window, *refs):
    sources, (table, scales), held, copied = refs[:5], refs[5:7], refs[7:12], refs[12]
    fetches = fetches_of(sources, held, copied)
    for fetch in fetches:
        fetch.start()
    for fetch in fetches:
        fetch.wait()
    columns, values, obs_weights, settling, weights = held
    lat, own = window_start(lat_count, rows, window)
    first = lat * rows - own
    slots, obs, lat_total = values.shape
    wide = -(-lat_total // LANES) * LANES
    low = lane_iota(obs) < HALF

    def windowed(array):
        if wide > lat_total:
            array = jnp.concatenate([array, jnp.zeros((obs, wide - lat_total), array.dtype)], axis=1)
        return pltpu.roll(array, lax.rem(wide - first, wide), 1)[:, :LANES]

    def paired(first_slot, second_slot):
        return jnp.where(low, windowed(first_slot), pltpu.roll(windowed(second_slot), HALF, 1))

    held = columns[...].astype(jnp.float32)
    place = paired(held, held)
    weight = paired(obs_weights[0], obs_weights[1])
    product = paired(obs_weights[0] * values[0], obs_weights[1] * values[1])
    sub = lax.broadcasted_iota(jnp.int32, (HALF, LANES), 0)
    start = lax.axis_index("lon") * cols - cols + lon_total
    here = lax.rem(sub + start, lon_total).astype(jnp.float32)
    sum_weight = jnp.zeros((HALF, LANES), jnp.float32)
    sum_product = jnp.zeros((HALF, LANES), jnp.float32)
    for index in range(obs):
        hit = here == place[index : index + 1]
        sum_weight += jnp.where(hit, weight[index : index + 1], 0.0)
        sum_product += jnp.where(hit, product[index : index + 1], 0.0)
    both = jnp.concatenate([sum_weight, sum_product], axis=0).T
    left, right = both[:window], both[HALF : HALF + window]
    low = lane_iota(window) < HALF
    table[0] = jnp.where(low, left, pltpu.roll(right, HALF, 1))
    table[1] = jnp.where(low, pltpu.roll(left, HALF, 1), right)
    levels, bins = settling.shape
    for k in range(levels):
        for size in range(bins):
            rate = settling[k : k + 1, size : size + 1]
            scales[k * bins + size] = jnp.broadcast_to(rate, (BLOCK, LANES))
    scales[levels * bins] = (BLOCK * BLOCK) * weight_rows(weights[...])


def rows_of(ref, field, window, spot):
    return ref[pl.ds(field * window + spot, EDGE, stride=window // EDGE), :]


def piece(field, window, spot):
    start = field * window + spot * EDGE
    return slice(start, start + EDGE)


def lay(lat_count, window, laid, place, block, rims):
    lat, own = window_start(lat_count, block.shape[0], window)
    rows = block.shape[0]

    def at(row, size):
        return pl.ds(pl.multiple_of(place * window + row, 8), size)

    if lat_count == 2:
        outer = lat * 2 * REACH
        laid[at(REACH, REACH)] = block[:REACH]
        laid[at(outer, REACH)] = block[REACH:]
        laid[at(2 * REACH - outer, REACH)] = rims[...]
    else:
        laid[at(own, rows)] = block[...]

        @pl.when(lat == 0)
        def _():
            laid[at(window - REACH, REACH)] = jnp.zeros((REACH, LANES), jnp.float32)

        @pl.when(lat == lat_count - 1)
        def _():
            laid[at(0, REACH)] = jnp.zeros((REACH, LANES), jnp.float32)

        @pl.when(lat > 0)
        def _():
            laid[at(own - REACH, REACH)] = rims[:REACH]

        @pl.when(lat < lat_count - 1)
        def _():
            laid[at(own + rows, REACH)] = rims[REACH:]


def near_is_west():
    return lax.rem(lax.axis_index("lon") + lax.axis_index("lev"), 2) == 1


def shares(block, place, bins, cols):
    lane = lane_iota(EDGE)
    low = lane < HALF
    zero = jnp.zeros((EDGE, LANES), jnp.float32)

    def turned(turn):
        return pltpu.roll(block, lax.rem(turn + 2 * LANES, LANES), 1)

    def inside(shift):
        from_start = lane - shift - place * cols
        return (from_start & (HALF - 1)) < cols

    out = [jnp.where(inside(0), turned((place - size) * cols), zero) for size in range(bins)]
    turn = (place - bins) * cols
    straight, crossed = turned(turn), turned(turn + HALF)
    out.append(jnp.where(inside(0), jnp.where(low, straight, crossed), zero))
    next_low = lax.rem(lane + LANES - 1, LANES) < HALF
    out.append(jnp.where(inside(1), jnp.where(next_low, turned(turn + 1), turned(turn + HALF + 1)), zero))
    out.append(jnp.where(inside(0), jnp.where(low, crossed, straight), zero))
    return out


def unpack_kernel(lat_count, bins, rows, cols, window, own_cells, near_cells, rims, begun, laid):
    levels = 2
    fields = levels * bins
    level = lax.axis_index("lev")
    for rank in range(levels):
        at = (rank + level) % levels
        lay(lat_count, window, laid, at * 2, own_cells.at[rank], rims.at[rank])
        lay(lat_count, window, laid, at * 2 + 1, near_cells.at[rank], rims.at[levels + rank])
    side = jnp.where(near_is_west(), 0, 2)
    for k in range(levels):
        for spot in range(window // EDGE):
            center = shares(rows_of(laid, 2 * k, window, spot), 1, bins, cols)
            beside = shares(rows_of(laid, 2 * k + 1, window, spot), side, bins, cols)
            both = [a + b for a, b in zip(center, beside)]
            for size in range(bins):
                begun[piece(k * bins + size, window, spot)] = both[size]
            wind, wind_next, mask = both[bins:]
            begun[piece(fields + 3 * k, window, spot)] = 1.0 - 4.0 * diffusion - wind
            begun[piece(fields + 3 * k + 1, window, spot)] = wind_next + diffusion
            begun[piece(fields + 3 * k + 2, window, spot)] = wind + diffusion
            if k == 0:
                begun[piece(fields + 3 * levels, window, spot)] = mask


def cycle_kernel(
    lat_count,
    slots,
    bins,
    rows,
    cols,
    window,
    begun,
    far,
    table,
    scales,
    trajectory,
    analysis_out,
    correction_out,
    fine,
    analysis,
    correction,
    coarse,
    change,
    winds,
    laid,
    copied,
    written,
):
    fetch = pltpu.make_async_copy(trajectory, fine, copied)
    fetch.start()
    levels = 2
    fields = levels * bins
    lat, own = window_start(lat_count, rows, window)
    level = lax.axis_index("lev")
    count = window // EDGE
    spots = range(count)
    for rank in range(levels):
        at = (rank + level) % levels
        lay(lat_count, window, laid, at, far.at[1 - rank, pl.ds(0, rows)], far.at[1 - rank, pl.ds(rows, window - rows)])
    side = jnp.where(near_is_west(), 2, 0)
    for k in range(levels):
        for spot in spots:
            share = shares(rows_of(laid, k, window, spot), side, bins, cols)
            for size in range(bins):
                at = piece(k * bins + size, window, spot)
                coarse[at] = begun[at] + share[size]
            wind, wind_next, mask_share = share[bins:]
            for index, value in enumerate((-wind, wind_next, wind)):
                winds[piece(3 * k + index, window, spot)] = begun[piece(fields + 3 * k + index, window, spot)] + value
            if k == 0:
                at = piece(3 * levels, window, spot)
                winds[at] = begun[piece(fields + 3 * levels, window, spot)] + mask_share

    sub = lax.broadcasted_iota(jnp.int32, (EDGE, LANES), 0)

    def carried(cells, k, backward):
        out = []
        for spot in spots:
            if spot:
                south = cells[spot - 1]
            else:
                south = jnp.where(sub == 0, 0.0, pltpu.roll(cells[-1], 1, 0))
            if spot < count - 1:
                north = cells[spot + 1]
            else:
                north = jnp.where(sub == EDGE - 1, 0.0, pltpu.roll(cells[0], EDGE - 1, 0))
            west, east = pltpu.roll(cells[spot], 1, 1), pltpu.roll(cells[spot], LANES - 1, 1)
            swept, other = (east, west) if backward else (west, east)
            near = diffusion * ((north + south) + other)
            out.append(
                (near + winds[piece(3 * k, window, spot)] * cells[spot])
                + winds[piece(3 * k + 1 + backward, window, spot)] * swept
            )
        return out

    def each(function, *lists):
        return [function(*values) for values in zip(*lists)]

    def added(first, second):
        return each(lambda a, b: a + b, first, second)

    def total_of(lists):
        out = lists[0]
        for values in lists[1:]:
            out = added(out, values)
        return out

    def scaled(factor, values):
        return [factor * value for value in values]

    def more(base, factor, values):
        return each(lambda a, b: a + factor * b, base, values)

    sizes = range(bins)
    upper = [scales[size, :1] for size in sizes]
    lower = [scales[bins + size, :1] for size in sizes]

    def summed_forward(top, bottom):
        sunk = [[] for _ in range(3)]
        cells = top
        for index in range(3):
            sunk[index] = [scaled(upper[size], cells[size]) for size in sizes]
            if index < 2:
                cells = [each(lambda a, b: a - b, carried(cells[size], 0, False), sunk[index][size]) for size in sizes]
        both = total_of(cells)
        both = each(lambda a, b: a - b, carried(both, 0, False), total_of(sunk[2]))
        both = carried(both, 0, False)
        factors = []
        for size in sizes:
            rate = -lower[size]
            first = scaled(rate, bottom[size])
            b3 = added(sunk[0][size], first)
            b2 = more(sunk[1][size], rate, b3)
            b1 = more(sunk[2][size], rate, b2)
            c0 = scaled(rate, b1)
            e3 = added(b3, first)
            e2 = more(b2, rate, e3)
            c1 = more(b1, rate, e2)
            f3 = added(e3, first)
            c2 = more(e2, rate, f3)
            c3 = added(f3, first)
            factors.append([c3, c2, c1, c0])
        moved = total_of(bottom)
        for index in range(4):
            moved = added(carried(moved, 1, False), total_of([factor[index] for factor in factors]))
        return added(both, moved)

    def spread_backward(start):
        powers = [start]
        for _ in range(4):
            powers.append(carried(powers[-1], 1, True))
        twice, thrice, thrice_more = scaled(2.0, powers[1]), scaled(3.0, powers[1]), scaled(3.0, powers[2])
        four, six, four_more = scaled(4.0, powers[1]), scaled(6.0, powers[2]), scaled(4.0, powers[3])
        first = carried(start, 0, True)
        second = carried(first, 0, True)
        gap = each(lambda a, b: a - b, powers[1], first)
        tops, bottoms = [], []
        for size in sizes:
            rate = -lower[size]
            low_two = more(powers[2], rate, more(twice, rate, start))
            low_three = more(powers[3], rate, more(thrice_more, rate, more(thrice, rate, start)))
            low_four = more(powers[4], rate, more(four_more, rate, more(six, rate, more(four, rate, start))))
            cells = more(second, upper[size], more(gap, rate, start))
            for below in (low_two, low_three):
                cells = more(carried(cells, 0, True), upper[size], each(lambda a, b: a - b, below, cells))
            tops.append(cells)
            bottoms.append(low_four)
        return tops + bottoms

    scale = 1.0 / fields
    mask = [winds[piece(3 * levels, window, spot)] for spot in spots]
    for field in range(fields):
        for spot in spots:
            change[piece(field, window, spot)] = jnp.zeros((EDGE, LANES), jnp.float32)

    def one_sweep(sweep, carry):
        cells = [[coarse[piece(field, window, spot)] for spot in spots] for field in range(fields)]
        if True:
            cells = [added(cells[field], [change[piece(field, window, spot)] for spot in spots]) for field in range(fields)]
        total = summed_forward(cells[:bins], cells[bins:])
        start = [
            rows_of(table, 0, window, spot) * (total[spot] * (scale * scale)) - rows_of(table, 1, window, spot) * scale
            for spot in spots
        ]
        adjoint = spread_backward(start)
        for field in range(fields):
            for spot in spots:
                if True:
                    old = change[piece(field, window, spot)]
                    value = old - step_length * (background * old + adjoint[field][spot])
                else:
                    value = -step_length * adjoint[field][spot]
                change[piece(field, window, spot)] = mask[spot] * value
        return carry

    lax.fori_loop(0, SWEEPS, one_sweep, 0)

    for field in range(fields):
        for spot in spots:
            coarse[pl.ds(field * window + spot, EDGE, stride=count), :] = change[piece(field, window, spot)]
    final = [
        coarse[pl.ds(pl.multiple_of((level * bins + size) * window + own, 8), rows)] for size in range(bins)
    ]
    for size in range(bins):
        turned = final[size].T
        for slot in range(slots):
            start = slot * HALF + cols
            correction[slot, size, 0] = turned[start : start + cols]
    writes = [pltpu.make_async_copy(correction, correction_out, written.at[slots * bins])]
    writes[0].start()
    source_lane = lax.broadcasted_iota(jnp.int32, (LANES, slots * LANES), 0)
    target_lane = lax.broadcasted_iota(jnp.int32, (LANES, slots * LANES), 1)
    picks = source_lane == target_lane // LANES * HALF + cols + target_lane % LANES // BLOCK
    picks = picks.astype(jnp.float32).astype(jnp.bfloat16)
    wide = jnp.dot(
        three_parts(jnp.concatenate(final)), jnp.concatenate([picks] * 3), preferred_element_type=jnp.float32
    )
    growth = scales[levels * bins]
    fetch.wait()
    for slot in range(slots):
        for size in range(bins):
            cells = wide[size * rows : (size + 1) * rows, slot * LANES : (slot + 1) * LANES]
            raised = (cells[:, None, :] * growth[None]).reshape(rows * BLOCK, LANES)
            analysis[slot, size, 0] = (fine[slot, size, 0].astype(jnp.float32) + raised).astype(jnp.bfloat16)
            at = (slot, size)
            writes.append(pltpu.make_async_copy(analysis.at[at], analysis_out.at[at], written.at[slot * bins + size]))
            writes[-1].start()
    for write in writes:
        write.wait()


def solution(mesh):
    lon_count, lat_count, lev_count = (mesh.shape[axis] for axis in AXES)

    def place_of(lon, lat, lev):
        return (lon % lon_count * lat_count + lat) * lev_count + lev

    def moved(values, source_of):
        pairs = []
        for lon in range(lon_count):
            for lat in range(lat_count):
                for lev in range(lev_count):
                    source = source_of(lon, lat, lev)
                    if source is not None:
                        pairs.append((place_of(*source), place_of(lon, lat, lev)))
        return lax.ppermute(values, AXES, pairs)

    def per_device(
        trajectory,
        block_weights,
        wind_speed,
        settling,
        source_mask,
        obs_columns,
        obs_values,
        obs_weights,
    ):
        slots, bins, _, fine_rows, fine_cols = trajectory.shape
        rows, cols = fine_rows // BLOCK, fine_cols // BLOCK
        rims = min(lat_count - 1, 2)
        window = rows + rims * REACH
        small = pltpu.CompilerParams(vmem_limit_bytes=8 * 1024 * 1024)
        in_vmem = pl.BlockSpec(memory_space=pltpu.VMEM)

        def kept(array):
            return pltpu.with_memory_space_constraint(array, pltpu.HBM)

        in_hbm = pl.BlockSpec(memory_space=pltpu.HBM)

        def restrict(*refs):
            restrict_kernel(lat_count, slots, bins, rows, cols, *refs)

        packed = pl.pallas_call(
            restrict,
            out_shape=pltpu.VMEM((rows, LANES), jnp.float32),
            in_specs=[in_hbm] * 4,
            out_specs=in_vmem,
            scratch_shapes=[
                pltpu.VMEM(trajectory.shape, jnp.bfloat16),
                pltpu.VMEM((BLOCK, BLOCK), jnp.float32),
                pltpu.VMEM((1, cols, rows), jnp.float32),
                pltpu.VMEM((cols, rows), jnp.int32),
                pltpu.VMEM((slots * bins * fine_rows, LANES), jnp.float32),
                pltpu.SemaphoreType.DMA((3 + slots * bins,)),
            ],
            compiler_params=small,
        )(*map(kept, (trajectory, block_weights, wind_speed.swapaxes(1, 2), source_mask.T)))

        def tabulate(*refs):
            obs_kernel(lat_count, lon_count * cols, rows, cols, window, *refs)

        observed = (
            obs_columns.T,
            obs_values.swapaxes(1, 2),
            obs_weights.swapaxes(1, 2),
            settling.T,
            block_weights,
        )
        table, scales = pl.pallas_call(
            tabulate,
            out_shape=(
                pltpu.VMEM((2, window, LANES), jnp.float32),
                pltpu.VMEM((2 * bins + 1, BLOCK, LANES), jnp.float32),
            ),
            in_specs=[in_hbm] * 5,
            out_specs=(in_vmem, in_vmem),
            scratch_shapes=[pltpu.VMEM(array.shape, array.dtype) for array in observed]
            + [pltpu.SemaphoreType.DMA((5,))],
            compiler_params=small,
        )(*map(kept, observed))

        own = jnp.stack([packed, moved(packed, lambda lon, lat, lev: (lon, lat, 1 - lev))])
        near = moved(own, lambda lon, lat, lev: (lon ^ 1 if lev == 0 else lon + 1 - 2 * ((lon + 1) % 2), lat, lev))
        near, table, scales = lax.optimization_barrier((near, table, scales))
        held = jnp.concatenate([own, near])
        if lat_count == 2:
            rims = moved(held[:, :REACH], lambda lon, lat, lev: (lon, 1 - lat, lev))
        else:
            low = moved(
                held[:, rows - REACH :], lambda lon, lat, lev: (lon, lat - 1, lev) if lat > 0 else None
            )
            high = moved(
                held[:, :REACH], lambda lon, lat, lev: (lon, lat + 1, lev) if lat < lat_count - 1 else None
            )
            rims = jnp.concatenate([low, high], axis=1)
        brought = jnp.concatenate([near, rims[2:]], axis=1)
        far = moved(brought, lambda lon, lat, lev: (lon, lat, 1 - lev))

        def cycle(*refs):
            cycle_kernel(lat_count, slots, bins, rows, cols, window, *refs)

        fields = 2 * bins
        fields = 2 * bins
        field_shape = ((fields + 7) * window, LANES)

        def unpack(*refs):
            unpack_kernel(lat_count, bins, rows, cols, window, *refs)

        begun = pl.pallas_call(
            unpack,
            out_shape=pltpu.VMEM(field_shape, jnp.float32),
            in_specs=[in_vmem] * 3,
            out_specs=in_vmem,
            scratch_shapes=[pltpu.VMEM((4 * window, LANES), jnp.float32)],
            compiler_params=small,
        )(own, near, rims)
        begun, far = lax.optimization_barrier((begun, far))
        field_store = pltpu.VMEM((fields * window, LANES), jnp.float32)
        analysis, correction = pl.pallas_call(
            cycle,
            out_shape=(
                jax.ShapeDtypeStruct(trajectory.shape, jnp.bfloat16),
                jax.ShapeDtypeStruct((slots, bins, 1, cols, rows), jnp.float32),
            ),
            in_specs=[in_vmem] * 4 + [in_hbm],
            out_specs=(in_hbm, in_hbm),
            scratch_shapes=[
                pltpu.VMEM(trajectory.shape, jnp.bfloat16),
                pltpu.VMEM(trajectory.shape, jnp.bfloat16),
                pltpu.VMEM((slots, bins, 1, cols, rows), jnp.float32),
                field_store,
                field_store,
                pltpu.VMEM((7 * window, LANES), jnp.float32),
                pltpu.VMEM((2 * window, LANES), jnp.float32),
                pltpu.SemaphoreType.DMA,
                pltpu.SemaphoreType.DMA((slots * bins + 1,)),
            ],
            compiler_params=small,
        )(begun, far, table.reshape(-1, LANES), scales, kept(trajectory))
        return analysis, correction.swapaxes(3, 4)

    placed = (
        P("member", None, "lev", "lat", "lon"),
        P(),
        P("lev", "lat", "lon"),
        P(),
        P("lat", "lon"),
        P("member", None),
        P("member", None, None),
        P("member", None, None),
    )
    return jax.shard_map(
        per_device,
        mesh=mesh,
        in_specs=placed,
        out_specs=(P("member", None, "lev", "lat", "lon"), P("member", None, "lev", "lat", "lon")),
        check_vma=False,
    )
```

```python
import jax
import jax.numpy as jnp
from jax import lax
from jax.experimental import pallas as pl
from jax.experimental.pallas import tpu as pltpu
from jax.sharding import PartitionSpec as P

BLOCK = 8
STEPS = 4
SWEEPS = 2
REACH = STEPS * 2 * SWEEPS
LANES = 128
HALF = LANES // 2
EDGE = 8

diffusion = 0.05
background = 0.1
step_length = 4.0
AXES = ("lon", "lat", "lev")


def lane_iota(rows):
    return lax.broadcasted_iota(jnp.int32, (rows, LANES), 1)


def three_parts(values):
    high = values.astype(jnp.bfloat16)
    rest = values - high.astype(jnp.float32)
    middle = rest.astype(jnp.bfloat16)
    low = (rest - middle.astype(jnp.float32)).astype(jnp.bfloat16)
    return jnp.concatenate([high, middle, low], axis=1)


def weight_rows(weights):
    return jnp.concatenate([weights] * (LANES // BLOCK), axis=1)


def fetches_of(sources, held, copied):
    return [
        pltpu.make_async_copy(source, target, copied.at[index])
        for index, (source, target) in enumerate(zip(sources, held))
    ]


def restrict_kernel(lat_count, slots, bins, rows, cols, *refs):
    sources, packed, held, fine, copied = refs[:4], refs[4], refs[5:9], refs[9], refs[10]
    trajectory, weights, wind, mask = held
    parts = [(slot, size) for slot in range(slots) for size in range(bins)]
    fetches = fetches_of(
        [*sources[1:], *(sources[0].at[at] for at in parts)],
        [*held[1:], *(trajectory.at[at] for at in parts)],
        copied,
    )
    for fetch in fetches:
        fetch.start()
    for fetch in fetches[:3]:
        fetch.wait()
    rows_of_weights = weight_rows(weights[...])
    row_sums = []
    for index, at in enumerate(parts):
        fetches[3 + index].wait()
        start = index * rows * BLOCK
        fine[start : start + rows * BLOCK] = trajectory[at].reshape(rows * BLOCK, LANES).astype(jnp.float32)
        total = fine[pl.ds(start, rows, stride=BLOCK), :] * rows_of_weights[:1]
        for row in range(1, BLOCK):
            total += fine[pl.ds(start + row, rows, stride=BLOCK), :] * rows_of_weights[row : row + 1]
        row_sums.append(total)
    row_sums = jnp.concatenate(row_sums)
    cell = lax.broadcasted_iota(jnp.int32, (LANES, LANES), 0) // BLOCK
    pool = (cell == lane_iota(LANES) % cols).astype(jnp.float32).astype(jnp.bfloat16)
    pooled = jnp.dot(three_parts(row_sums), jnp.concatenate([pool] * 3), preferred_element_type=jnp.float32)
    group = lane_iota(rows) // cols
    filler = jnp.zeros((bins * cols, rows), jnp.float32)
    out = jnp.concatenate([filler, wind[0], filler, mask[...].astype(jnp.float32)], axis=0).T
    for slot in range(slots):
        for size in range(bins):
            start = (slot * bins + size) * rows
            out = jnp.where(
                group == slot * (bins + 1) + size, pooled[start : start + rows], out
            )
    if lat_count == 2:
        start = pl.multiple_of(jnp.where(lax.axis_index("lat") == 0, rows - REACH, 0), 8)
        packed[pl.ds(start, REACH)] = out[:REACH]
        packed[pl.ds(pl.multiple_of(rows - REACH - start, 8), REACH)] = out[REACH:]
    else:
        packed[...] = out


def window_start(lat_count, rows, window):
    lat = lax.axis_index("lat")
    own = jnp.where(lat == 0, 0, jnp.where(lat == lat_count - 1, window - rows, REACH))
    return lat, own


def obs_kernel(lat_count, lon_total, rows, cols, window, *refs):
    sources, (table, scales), held, copied = refs[:5], refs[5:7], refs[7:12], refs[12]
    fetches = fetches_of(sources, held, copied)
    for fetch in fetches:
        fetch.start()
    for fetch in fetches:
        fetch.wait()
    columns, values, obs_weights, settling, weights = held
    lat, own = window_start(lat_count, rows, window)
    first = lat * rows - own
    slots, obs, lat_total = values.shape
    wide = -(-lat_total // LANES) * LANES
    low = lane_iota(obs) < HALF

    def windowed(array):
        if wide > lat_total:
            array = jnp.concatenate([array, jnp.zeros((obs, wide - lat_total), array.dtype)], axis=1)
        return pltpu.roll(array, lax.rem(wide - first, wide), 1)[:, :LANES]

    def paired(first_slot, second_slot):
        return jnp.where(low, windowed(first_slot), pltpu.roll(windowed(second_slot), HALF, 1))

    held = columns[...].astype(jnp.float32)
    place = paired(held, held)
    weight = paired(obs_weights[0], obs_weights[1])
    product = paired(obs_weights[0] * values[0], obs_weights[1] * values[1])
    sub = lax.broadcasted_iota(jnp.int32, (HALF, LANES), 0)
    start = lax.axis_index("lon") * cols - cols + lon_total
    here = lax.rem(sub + start, lon_total).astype(jnp.float32)
    sum_weight = jnp.zeros((HALF, LANES), jnp.float32)
    sum_product = jnp.zeros((HALF, LANES), jnp.float32)
    for index in range(obs):
        hit = here == place[index : index + 1]
        sum_weight += jnp.where(hit, weight[index : index + 1], 0.0)
        sum_product += jnp.where(hit, product[index : index + 1], 0.0)
    both = jnp.concatenate([sum_weight, sum_product], axis=0).T
    left, right = both[:window], both[HALF : HALF + window]
    low = lane_iota(window) < HALF
    table[0] = jnp.where(low, left, pltpu.roll(right, HALF, 1))
    table[1] = jnp.where(low, pltpu.roll(left, HALF, 1), right)
    levels, bins = settling.shape
    for k in range(levels):
        for size in range(bins):
            rate = settling[k : k + 1, size : size + 1]
            scales[k * bins + size] = jnp.broadcast_to(rate, (BLOCK, LANES))
    scales[levels * bins] = (BLOCK * BLOCK) * weight_rows(weights[...])


def rows_of(ref, field, window, spot):
    return ref[pl.ds(field * window + spot, EDGE, stride=window // EDGE), :]


def piece(field, window, spot):
    start = field * window + spot * EDGE
    return slice(start, start + EDGE)


def lay(lat_count, window, laid, place, block, rims):
    lat, own = window_start(lat_count, block.shape[0], window)
    rows = block.shape[0]

    def at(row, size):
        return pl.ds(pl.multiple_of(place * window + row, 8), size)

    if lat_count == 2:
        outer = lat * 2 * REACH
        laid[at(REACH, REACH)] = block[:REACH]
        laid[at(outer, REACH)] = block[REACH:]
        laid[at(2 * REACH - outer, REACH)] = rims[...]
    else:
        laid[at(own, rows)] = block[...]

        @pl.when(lat == 0)
        def _():
            laid[at(window - REACH, REACH)] = jnp.zeros((REACH, LANES), jnp.float32)

        @pl.when(lat == lat_count - 1)
        def _():
            laid[at(0, REACH)] = jnp.zeros((REACH, LANES), jnp.float32)

        @pl.when(lat > 0)
        def _():
            laid[at(own - REACH, REACH)] = rims[:REACH]

        @pl.when(lat < lat_count - 1)
        def _():
            laid[at(own + rows, REACH)] = rims[REACH:]


def near_is_west():
    return lax.rem(lax.axis_index("lon") + lax.axis_index("lev"), 2) == 1


def shares(block, place, bins, cols):
    lane = lane_iota(EDGE)
    low = lane < HALF
    zero = jnp.zeros((EDGE, LANES), jnp.float32)

    def turned(turn):
        return pltpu.roll(block, lax.rem(turn + 2 * LANES, LANES), 1)

    def inside(shift):
        from_start = lane - shift - place * cols
        return (from_start & (HALF - 1)) < cols

    out = [jnp.where(inside(0), turned((place - size) * cols), zero) for size in range(bins)]
    turn = (place - bins) * cols
    straight, crossed = turned(turn), turned(turn + HALF)
    out.append(jnp.where(inside(0), jnp.where(low, straight, crossed), zero))
    next_low = lax.rem(lane + LANES - 1, LANES) < HALF
    out.append(jnp.where(inside(1), jnp.where(next_low, turned(turn + 1), turned(turn + HALF + 1)), zero))
    out.append(jnp.where(inside(0), jnp.where(low, crossed, straight), zero))
    return out


def unpack_kernel(lat_count, bins, rows, cols, window, own_cells, near_cells, rims, begun, laid):
    levels = 2
    fields = levels * bins
    level = lax.axis_index("lev")
    for rank in range(levels):
        at = (rank + level) % levels
        lay(lat_count, window, laid, at * 2, own_cells.at[rank], rims.at[rank])
        lay(lat_count, window, laid, at * 2 + 1, near_cells.at[rank], rims.at[levels + rank])
    side = jnp.where(near_is_west(), 0, 2)
    for k in range(levels):
        for spot in range(window // EDGE):
            center = shares(rows_of(laid, 2 * k, window, spot), 1, bins, cols)
            beside = shares(rows_of(laid, 2 * k + 1, window, spot), side, bins, cols)
            both = [a + b for a, b in zip(center, beside)]
            for size in range(bins):
                begun[piece(k * bins + size, window, spot)] = both[size]
            wind, wind_next, mask = both[bins:]
            begun[piece(fields + 3 * k, window, spot)] = 1.0 - 4.0 * diffusion - wind
            begun[piece(fields + 3 * k + 1, window, spot)] = wind_next + diffusion
            begun[piece(fields + 3 * k + 2, window, spot)] = wind + diffusion
            if k == 0:
                begun[piece(fields + 3 * levels, window, spot)] = mask


def cycle_kernel(
    lat_count,
    slots,
    bins,
    rows,
    cols,
    window,
    begun,
    far,
    table,
    scales,
    trajectory,
    analysis_out,
    correction_out,
    fine,
    analysis,
    correction,
    coarse,
    change,
    winds,
    laid,
    copied,
    written,
):
    fetch = pltpu.make_async_copy(trajectory, fine, copied)
    fetch.start()
    levels = 2
    fields = levels * bins
    lat, own = window_start(lat_count, rows, window)
    level = lax.axis_index("lev")
    count = window // EDGE
    spots = range(count)
    for rank in range(levels):
        at = (rank + level) % levels
        lay(lat_count, window, laid, at, far.at[1 - rank, pl.ds(0, rows)], far.at[1 - rank, pl.ds(rows, window - rows)])
    side = jnp.where(near_is_west(), 2, 0)
    for k in range(levels):
        for spot in spots:
            share = shares(rows_of(laid, k, window, spot), side, bins, cols)
            for size in range(bins):
                at = piece(k * bins + size, window, spot)
                coarse[at] = begun[at] + share[size]
            wind, wind_next, mask_share = share[bins:]
            stay, next_sweep, sweep = (
                begun[piece(fields + 3 * k + index, window, spot)] + value
                for index, value in enumerate((-wind, wind_next, wind))
            )
            last_sweep, over_sweep = pltpu.roll(sweep, LANES - 1, 1), pltpu.roll(next_sweep, 1, 1)
            kept = 1.0 - 3.0 * diffusion
            for index, value in enumerate(
                (kept - last_sweep, stay, kept - next_sweep, last_sweep, sweep, next_sweep, over_sweep)
            ):
                winds[piece(7 * k + index, window, spot)] = value
            if k == 0:
                winds[piece(7 * levels, window, spot)] = begun[piece(fields + 3 * levels, window, spot)] + mask_share

    sub = lax.broadcasted_iota(jnp.int32, (EDGE, LANES), 0)

    def copies(cells, reach):
        out = {0: cells}
        for turn in range(1, reach + 1):
            out[turn] = [pltpu.roll(value, turn, 1) for value in cells]
            out[-turn] = [pltpu.roll(value, LANES - turn, 1) for value in cells]
        return out

    def carried_at(turned, k, backward, turn):
        cells, west, east = turned[turn], turned[turn + 1], turned[turn - 1]
        out = []
        for spot in spots:
            if spot:
                south = cells[spot - 1]
            else:
                south = jnp.where(sub == 0, 0.0, pltpu.roll(cells[-1], 1, 0))
            if spot < count - 1:
                north = cells[spot + 1]
            else:
                north = jnp.where(sub == EDGE - 1, 0.0, pltpu.roll(cells[0], EDGE - 1, 0))
            swept, other = (east[spot], west[spot]) if backward else (west[spot], east[spot])
            near = diffusion * ((north + south) + other)
            sweep = 7 * k + 4 + turn + (not backward)
            out.append(
                (near + winds[piece(7 * k + 1 + turn, window, spot)] * cells[spot])
                + winds[piece(sweep, window, spot)] * swept
            )
        return out

    def carried(cells, k, backward):
        return carried_at(copies(cells, 1), k, backward, 0)

    def each(function, *lists):
        return [function(*values) for values in zip(*lists)]

    def added(first, second):
        return each(lambda a, b: a + b, first, second)

    def total_of(lists):
        out = lists[0]
        for values in lists[1:]:
            out = added(out, values)
        return out

    def scaled(factor, values):
        return [factor * value for value in values]

    def more(base, factor, values):
        return each(lambda a, b: a + factor * b, base, values)

    sizes = range(bins)
    upper = [scales[size, :1] for size in sizes]
    lower = [scales[bins + size, :1] for size in sizes]

    def summed_forward(top, bottom):
        sunk = [[] for _ in range(3)]
        cells = top
        for index in range(3):
            sunk[index] = [scaled(upper[size], cells[size]) for size in sizes]
            if index < 2:
                cells = [each(lambda a, b: a - b, carried(cells[size], 0, False), sunk[index][size]) for size in sizes]
        turned, sinking = copies(total_of(cells), 2), copies(total_of(sunk[2]), 1)
        both = {
            turn: each(lambda a, b: a - b, carried_at(turned, 0, False, turn), sinking[turn]) for turn in (-1, 0, 1)
        }
        both = carried_at(both, 0, False, 0)
        factors = []
        for size in sizes:
            rate = -lower[size]
            first = scaled(rate, bottom[size])
            b3 = added(sunk[0][size], first)
            b2 = more(sunk[1][size], rate, b3)
            b1 = more(sunk[2][size], rate, b2)
            c0 = scaled(rate, b1)
            e3 = added(b3, first)
            e2 = more(b2, rate, e3)
            c1 = more(b1, rate, e2)
            f3 = added(e3, first)
            c2 = more(e2, rate, f3)
            c3 = added(f3, first)
            factors.append([c3, c2, c1, c0])
        moved = total_of(bottom)
        sums = [total_of([factor[index] for factor in factors]) for index in range(4)]
        for index in range(2):
            moved = added(carried(moved, 1, False), sums[index])
        turned, third = copies(moved, 2), copies(sums[2], 1)
        moved = {turn: added(carried_at(turned, 1, False, turn), third[turn]) for turn in (-1, 0, 1)}
        return added(both, added(carried_at(moved, 1, False, 0), sums[3]))

    def spread_backward(start):
        turned = copies(start, 2)
        lower_one, upper_one = (
            {turn: carried_at(turned, k, True, turn) for turn in (-1, 0, 1)} for k in (1, 0)
        )
        powers = [start, lower_one[0], carried_at(lower_one, 1, True, 0)]
        for _ in range(2):
            powers.append(carried(powers[-1], 1, True))
        twice, thrice, thrice_more = scaled(2.0, powers[1]), scaled(3.0, powers[1]), scaled(3.0, powers[2])
        four, six, four_more = scaled(4.0, powers[1]), scaled(6.0, powers[2]), scaled(4.0, powers[3])
        first, second = upper_one[0], carried_at(upper_one, 0, True, 0)
        gap = each(lambda a, b: a - b, powers[1], first)
        tops, bottoms = [], []
        for size in sizes:
            rate = -lower[size]
            low_two = more(powers[2], rate, more(twice, rate, start))
            low_three = more(powers[3], rate, more(thrice_more, rate, more(thrice, rate, start)))
            low_four = more(powers[4], rate, more(four_more, rate, more(six, rate, more(four, rate, start))))
            cells = more(second, upper[size], more(gap, rate, start))
            for below in (low_two, low_three):
                cells = more(carried(cells, 0, True), upper[size], each(lambda a, b: a - b, below, cells))
            tops.append(cells)
            bottoms.append(low_four)
        return tops + bottoms

    scale = 1.0 / fields
    mask = [winds[piece(7 * levels, window, spot)] for spot in spots]
    for field in range(fields):
        for spot in spots:
            change[piece(field, window, spot)] = jnp.zeros((EDGE, LANES), jnp.float32)

    def one_sweep(sweep, carry):
        cells = [[coarse[piece(field, window, spot)] for spot in spots] for field in range(fields)]
        if True:
            cells = [added(cells[field], [change[piece(field, window, spot)] for spot in spots]) for field in range(fields)]
        total = summed_forward(cells[:bins], cells[bins:])
        start = [
            rows_of(table, 0, window, spot) * (total[spot] * (scale * scale)) - rows_of(table, 1, window, spot) * scale
            for spot in spots
        ]
        adjoint = spread_backward(start)
        for field in range(fields):
            for spot in spots:
                if True:
                    old = change[piece(field, window, spot)]
                    value = old - step_length * (background * old + adjoint[field][spot])
                else:
                    value = -step_length * adjoint[field][spot]
                change[piece(field, window, spot)] = mask[spot] * value
        return carry

    lax.fori_loop(0, SWEEPS, one_sweep, 0)

    for field in range(fields):
        for spot in spots:
            coarse[pl.ds(field * window + spot, EDGE, stride=count), :] = change[piece(field, window, spot)]
    final = [
        coarse[pl.ds(pl.multiple_of((level * bins + size) * window + own, 8), rows)] for size in range(bins)
    ]
    for size in range(bins):
        turned = final[size].T
        for slot in range(slots):
            start = slot * HALF + cols
            correction[slot, size, 0] = turned[start : start + cols]
    writes = [pltpu.make_async_copy(correction, correction_out, written.at[slots * bins])]
    writes[0].start()
    source_lane = lax.broadcasted_iota(jnp.int32, (LANES, slots * LANES), 0)
    target_lane = lax.broadcasted_iota(jnp.int32, (LANES, slots * LANES), 1)
    picks = source_lane == target_lane // LANES * HALF + cols + target_lane % LANES // BLOCK
    picks = picks.astype(jnp.float32).astype(jnp.bfloat16)
    wide = jnp.dot(
        three_parts(jnp.concatenate(final)), jnp.concatenate([picks] * 3), preferred_element_type=jnp.float32
    )
    growth = scales[levels * bins]
    fetch.wait()
    for slot in range(slots):
        for size in range(bins):
            cells = wide[size * rows : (size + 1) * rows, slot * LANES : (slot + 1) * LANES]
            raised = (cells[:, None, :] * growth[None]).reshape(rows * BLOCK, LANES)
            analysis[slot, size, 0] = (fine[slot, size, 0].astype(jnp.float32) + raised).astype(jnp.bfloat16)
            at = (slot, size)
            writes.append(pltpu.make_async_copy(analysis.at[at], analysis_out.at[at], written.at[slot * bins + size]))
            writes[-1].start()
    for write in writes:
        write.wait()


def solution(mesh):
    lon_count, lat_count, lev_count = (mesh.shape[axis] for axis in AXES)

    def place_of(lon, lat, lev):
        return (lon % lon_count * lat_count + lat) * lev_count + lev

    def moved(values, source_of):
        pairs = []
        for lon in range(lon_count):
            for lat in range(lat_count):
                for lev in range(lev_count):
                    source = source_of(lon, lat, lev)
                    if source is not None:
                        pairs.append((place_of(*source), place_of(lon, lat, lev)))
        return lax.ppermute(values, AXES, pairs)

    def per_device(
        trajectory,
        block_weights,
        wind_speed,
        settling,
        source_mask,
        obs_columns,
        obs_values,
        obs_weights,
    ):
        slots, bins, _, fine_rows, fine_cols = trajectory.shape
        rows, cols = fine_rows // BLOCK, fine_cols // BLOCK
        rims = min(lat_count - 1, 2)
        window = rows + rims * REACH
        small = pltpu.CompilerParams(vmem_limit_bytes=8 * 1024 * 1024)
        in_vmem = pl.BlockSpec(memory_space=pltpu.VMEM)

        def kept(array):
            return pltpu.with_memory_space_constraint(array, pltpu.HBM)

        in_hbm = pl.BlockSpec(memory_space=pltpu.HBM)

        def restrict(*refs):
            restrict_kernel(lat_count, slots, bins, rows, cols, *refs)

        packed = pl.pallas_call(
            restrict,
            out_shape=pltpu.VMEM((rows, LANES), jnp.float32),
            in_specs=[in_hbm] * 4,
            out_specs=in_vmem,
            scratch_shapes=[
                pltpu.VMEM(trajectory.shape, jnp.bfloat16),
                pltpu.VMEM((BLOCK, BLOCK), jnp.float32),
                pltpu.VMEM((1, cols, rows), jnp.float32),
                pltpu.VMEM((cols, rows), jnp.int32),
                pltpu.VMEM((slots * bins * fine_rows, LANES), jnp.float32),
                pltpu.SemaphoreType.DMA((3 + slots * bins,)),
            ],
            compiler_params=small,
        )(*map(kept, (trajectory, block_weights, wind_speed.swapaxes(1, 2), source_mask.T)))

        def tabulate(*refs):
            obs_kernel(lat_count, lon_count * cols, rows, cols, window, *refs)

        observed = (
            obs_columns.T,
            obs_values.swapaxes(1, 2),
            obs_weights.swapaxes(1, 2),
            settling.T,
            block_weights,
        )
        table, scales = pl.pallas_call(
            tabulate,
            out_shape=(
                pltpu.VMEM((2, window, LANES), jnp.float32),
                pltpu.VMEM((2 * bins + 1, BLOCK, LANES), jnp.float32),
            ),
            in_specs=[in_hbm] * 5,
            out_specs=(in_vmem, in_vmem),
            scratch_shapes=[pltpu.VMEM(array.shape, array.dtype) for array in observed]
            + [pltpu.SemaphoreType.DMA((5,))],
            compiler_params=small,
        )(*map(kept, observed))

        own = jnp.stack([packed, moved(packed, lambda lon, lat, lev: (lon, lat, 1 - lev))])
        near = moved(own, lambda lon, lat, lev: (lon ^ 1 if lev == 0 else lon + 1 - 2 * ((lon + 1) % 2), lat, lev))
        near, table, scales = lax.optimization_barrier((near, table, scales))
        held = jnp.concatenate([own, near])
        if lat_count == 2:
            rims = moved(held[:, :REACH], lambda lon, lat, lev: (lon, 1 - lat, lev))
        else:
            low = moved(
                held[:, rows - REACH :], lambda lon, lat, lev: (lon, lat - 1, lev) if lat > 0 else None
            )
            high = moved(
                held[:, :REACH], lambda lon, lat, lev: (lon, lat + 1, lev) if lat < lat_count - 1 else None
            )
            rims = jnp.concatenate([low, high], axis=1)
        brought = jnp.concatenate([near, rims[2:]], axis=1)
        far = moved(brought, lambda lon, lat, lev: (lon, lat, 1 - lev))

        def cycle(*refs):
            cycle_kernel(lat_count, slots, bins, rows, cols, window, *refs)

        fields = 2 * bins
        fields = 2 * bins
        field_shape = ((fields + 7) * window, LANES)

        def unpack(*refs):
            unpack_kernel(lat_count, bins, rows, cols, window, *refs)

        begun = pl.pallas_call(
            unpack,
            out_shape=pltpu.VMEM(field_shape, jnp.float32),
            in_specs=[in_vmem] * 3,
            out_specs=in_vmem,
            scratch_shapes=[pltpu.VMEM((4 * window, LANES), jnp.float32)],
            compiler_params=small,
        )(own, near, rims)
        begun, far = lax.optimization_barrier((begun, far))
        field_store = pltpu.VMEM((fields * window, LANES), jnp.float32)
        analysis, correction = pl.pallas_call(
            cycle,
            out_shape=(
                jax.ShapeDtypeStruct(trajectory.shape, jnp.bfloat16),
                jax.ShapeDtypeStruct((slots, bins, 1, cols, rows), jnp.float32),
            ),
            in_specs=[in_vmem] * 4 + [in_hbm],
            out_specs=(in_hbm, in_hbm),
            scratch_shapes=[
                pltpu.VMEM(trajectory.shape, jnp.bfloat16),
                pltpu.VMEM(trajectory.shape, jnp.bfloat16),
                pltpu.VMEM((slots, bins, 1, cols, rows), jnp.float32),
                field_store,
                field_store,
                pltpu.VMEM((15 * window, LANES), jnp.float32),
                pltpu.VMEM((2 * window, LANES), jnp.float32),
                pltpu.SemaphoreType.DMA,
                pltpu.SemaphoreType.DMA((slots * bins + 1,)),
            ],
            compiler_params=small,
        )(begun, far, table.reshape(-1, LANES), scales, kept(trajectory))
        return analysis, correction.swapaxes(3, 4)

    placed = (
        P("member", None, "lev", "lat", "lon"),
        P(),
        P("lev", "lat", "lon"),
        P(),
        P("lat", "lon"),
        P("member", None),
        P("member", None, None),
        P("member", None, None),
    )
    return jax.shard_map(
        per_device,
        mesh=mesh,
        in_specs=placed,
        out_specs=(P("member", None, "lev", "lat", "lon"), P("member", None, "lev", "lat", "lon")),
        check_vma=False,
    )
```

```python
import jax
import jax.numpy as jnp
from jax import lax
from jax.experimental import pallas as pl
from jax.experimental.pallas import tpu as pltpu
from jax.sharding import PartitionSpec as P

BLOCK = 8
STEPS = 4
SWEEPS = 2
REACH = STEPS * 2 * SWEEPS
LANES = 128
HALF = LANES // 2
EDGE = 8

diffusion = 0.05
background = 0.1
step_length = 4.0
AXES = ("lon", "lat", "lev")


def lane_iota(rows):
    return lax.broadcasted_iota(jnp.int32, (rows, LANES), 1)


def three_parts(values):
    high = values.astype(jnp.bfloat16)
    rest = values - high.astype(jnp.float32)
    middle = rest.astype(jnp.bfloat16)
    low = (rest - middle.astype(jnp.float32)).astype(jnp.bfloat16)
    return jnp.concatenate([high, middle, low], axis=1)


def weight_rows(weights):
    return jnp.concatenate([weights] * (LANES // BLOCK), axis=1)


def fetches_of(sources, held, copied):
    return [
        pltpu.make_async_copy(source, target, copied.at[index])
        for index, (source, target) in enumerate(zip(sources, held))
    ]


def restrict_kernel(lat_count, slots, bins, rows, cols, *refs):
    sources, packed, held, fine, copied = refs[:4], refs[4], refs[5:9], refs[9], refs[10]
    trajectory, weights, wind, mask = held
    parts = [(slot, size) for slot in range(slots) for size in range(bins)]
    fetches = fetches_of(
        [*sources[1:], *(sources[0].at[at] for at in parts)],
        [*held[1:], *(trajectory.at[at] for at in parts)],
        copied,
    )
    for fetch in fetches:
        fetch.start()
    for fetch in fetches[:3]:
        fetch.wait()
    rows_of_weights = weight_rows(weights[...])
    row_sums = []
    for index, at in enumerate(parts):
        fetches[3 + index].wait()
        start = index * rows * BLOCK
        fine[start : start + rows * BLOCK] = trajectory[at].reshape(rows * BLOCK, LANES).astype(jnp.float32)
        total = fine[pl.ds(start, rows, stride=BLOCK), :] * rows_of_weights[:1]
        for row in range(1, BLOCK):
            total += fine[pl.ds(start + row, rows, stride=BLOCK), :] * rows_of_weights[row : row + 1]
        row_sums.append(total)
    row_sums = jnp.concatenate(row_sums)
    cell = lax.broadcasted_iota(jnp.int32, (LANES, LANES), 0) // BLOCK
    pool = (cell == lane_iota(LANES) % cols).astype(jnp.float32).astype(jnp.bfloat16)
    pooled = jnp.dot(three_parts(row_sums), jnp.concatenate([pool] * 3), preferred_element_type=jnp.float32)
    group = lane_iota(rows) // cols
    filler = jnp.zeros((bins * cols, rows), jnp.float32)
    out = jnp.concatenate([filler, wind[0], filler, mask[...].astype(jnp.float32)], axis=0).T
    for slot in range(slots):
        for size in range(bins):
            start = (slot * bins + size) * rows
            out = jnp.where(
                group == slot * (bins + 1) + size, pooled[start : start + rows], out
            )
    if lat_count == 2:
        start = pl.multiple_of(jnp.where(lax.axis_index("lat") == 0, rows - REACH, 0), 8)
        packed[pl.ds(start, REACH)] = out[:REACH]
        packed[pl.ds(pl.multiple_of(rows - REACH - start, 8), REACH)] = out[REACH:]
    else:
        packed[...] = out


def window_start(lat_count, rows, window):
    lat = lax.axis_index("lat")
    own = jnp.where(lat == 0, 0, jnp.where(lat == lat_count - 1, window - rows, REACH))
    return lat, own


def obs_kernel(lat_count, lon_total, rows, cols, window, *refs):
    sources, (table, scales), held, copied = refs[:5], refs[5:7], refs[7:12], refs[12]
    fetches = fetches_of(sources, held, copied)
    for fetch in fetches:
        fetch.start()
    for fetch in fetches:
        fetch.wait()
    columns, values, obs_weights, settling, weights = held
    lat, own = window_start(lat_count, rows, window)
    first = lat * rows - own
    slots, obs, lat_total = values.shape
    wide = -(-lat_total // LANES) * LANES
    low = lane_iota(obs) < HALF

    def windowed(array):
        if wide > lat_total:
            array = jnp.concatenate([array, jnp.zeros((obs, wide - lat_total), array.dtype)], axis=1)
        return pltpu.roll(array, lax.rem(wide - first, wide), 1)[:, :LANES]

    def paired(first_slot, second_slot):
        return jnp.where(low, windowed(first_slot), pltpu.roll(windowed(second_slot), HALF, 1))

    held = columns[...].astype(jnp.float32)
    place = paired(held, held)
    weight = paired(obs_weights[0], obs_weights[1])
    product = paired(obs_weights[0] * values[0], obs_weights[1] * values[1])
    sub = lax.broadcasted_iota(jnp.int32, (HALF, LANES), 0)
    start = lax.axis_index("lon") * cols - cols + lon_total
    here = lax.rem(sub + start, lon_total).astype(jnp.float32)
    sum_weight = jnp.zeros((HALF, LANES), jnp.float32)
    sum_product = jnp.zeros((HALF, LANES), jnp.float32)
    for index in range(obs):
        hit = here == place[index : index + 1]
        sum_weight += jnp.where(hit, weight[index : index + 1], 0.0)
        sum_product += jnp.where(hit, product[index : index + 1], 0.0)
    both = jnp.concatenate([sum_weight, sum_product], axis=0).T
    left, right = both[:window], both[HALF : HALF + window]
    low = lane_iota(window) < HALF
    table[0] = jnp.where(low, left, pltpu.roll(right, HALF, 1))
    table[1] = jnp.where(low, pltpu.roll(left, HALF, 1), right)
    levels, bins = settling.shape
    for k in range(levels):
        for size in range(bins):
            rate = settling[k : k + 1, size : size + 1]
            scales[k * bins + size] = jnp.broadcast_to(rate, (BLOCK, LANES))
    scales[levels * bins] = (BLOCK * BLOCK) * weight_rows(weights[...])


def rows_of(ref, field, window, spot):
    return ref[pl.ds(field * window + spot, EDGE, stride=window // EDGE), :]


def piece(field, window, spot):
    start = field * window + spot * EDGE
    return slice(start, start + EDGE)


def lay_block(lat_count, window, rows, store):
    lat, own = window_start(lat_count, rows, window)
    if lat_count == 2:
        store(0, REACH, REACH)
        store(REACH, rows - REACH, lat * 2 * REACH)
    else:
        store(0, rows, own)


def lay_rims(lat_count, window, rows, store):
    lat, own = window_start(lat_count, rows, window)
    if lat_count == 2:
        store(0, REACH, 2 * REACH - lat * 2 * REACH)
    else:
        pl.when(lat > 0)(lambda: store(0, REACH, own - REACH))
        pl.when(lat < lat_count - 1)(lambda: store(REACH, REACH, own + rows))


def near_is_west():
    return lax.rem(lax.axis_index("lon") + lax.axis_index("lev"), 2) == 1


def shares(block, place, bins, cols):
    lane = lane_iota(EDGE)
    low = lane < HALF
    zero = jnp.zeros((EDGE, LANES), jnp.float32)

    def turned(turn):
        return pltpu.roll(block, lax.rem(turn + 2 * LANES, LANES), 1)

    def inside(shift):
        from_start = lane - shift - place * cols
        return (from_start & (HALF - 1)) < cols

    out = [jnp.where(inside(0), turned((place - size) * cols), zero) for size in range(bins)]
    turn = (place - bins) * cols
    straight, crossed = turned(turn), turned(turn + HALF)
    out.append(jnp.where(inside(0), jnp.where(low, straight, crossed), zero))
    next_low = lax.rem(lane + LANES - 1, LANES) < HALF
    out.append(jnp.where(inside(1), jnp.where(next_low, turned(turn + 1), turned(turn + HALF + 1)), zero))
    out.append(jnp.where(inside(0), jnp.where(low, crossed, straight), zero))
    return out


def unpack_kernel(lat_count, bins, rows, cols, window, own_cells, near_cells, rims, begun, laid):
    levels = 2
    fields = levels * bins
    level = lax.axis_index("lev")
    laid[...] = jnp.zeros(laid.shape, jnp.float32)
    for rank in range(levels):
        at = (rank + level) % levels

        def store_of(block, place):
            def store(start, size, row):
                laid[pl.ds(pl.multiple_of(place * window + row, 8), size)] = block[pl.ds(start, size)]

            return store

        lay_block(lat_count, window, rows, store_of(own_cells.at[rank], at * 2))
        lay_block(lat_count, window, rows, store_of(near_cells.at[rank], at * 2 + 1))
        if rank == 0:
            lay_rims(lat_count, window, rows, store_of(rims.at[0], at * 2))
        lay_rims(lat_count, window, rows, store_of(rims.at[1 + rank], at * 2 + 1))
    side = jnp.where(near_is_west(), 0, 2)
    for k in range(levels):
        for spot in range(window // EDGE):
            center = shares(rows_of(laid, 2 * k, window, spot), 1, bins, cols)
            beside = shares(rows_of(laid, 2 * k + 1, window, spot), side, bins, cols)
            both = [a + b for a, b in zip(center, beside)]
            for size in range(bins):
                begun[piece(k * bins + size, window, spot)] = both[size]
            wind, wind_next, mask = both[bins:]
            begun[piece(fields + 3 * k, window, spot)] = 1.0 - 4.0 * diffusion - wind
            begun[piece(fields + 3 * k + 1, window, spot)] = wind_next + diffusion
            begun[piece(fields + 3 * k + 2, window, spot)] = wind + diffusion
            if k == 0:
                begun[piece(fields + 3 * levels, window, spot)] = mask


def cycle_kernel(
    lat_count,
    slots,
    bins,
    rows,
    cols,
    window,
    begun,
    far,
    table,
    scales,
    trajectory,
    analysis_out,
    correction_out,
    fine,
    analysis,
    correction,
    coarse,
    change,
    winds,
    laid,
    copied,
    written,
):
    fetch = pltpu.make_async_copy(trajectory, fine, copied)
    fetch.start()
    levels = 2
    fields = levels * bins
    lat, own = window_start(lat_count, rows, window)
    level = lax.axis_index("lev")
    count = window // EDGE
    spots = range(count)
    kinds = bins + 3
    side = jnp.where(near_is_west(), 2, 0)
    if lat_count != 2:
        laid[...] = jnp.zeros(laid.shape, jnp.float32)

    def store_of(first, at, place, more_to):
        def store(start, size, row):
            for part in range(0, size, EDGE):
                share = shares(far[pl.ds(first + start + part, EDGE)], place, bins, cols)
                for kind in range(kinds):
                    target = (at * kinds + kind) * window + row + part
                    target = pl.ds(pl.multiple_of(target, 8), EDGE)
                    laid[target] = laid[target] + share[kind] if more_to else share[kind]

        return store

    height = window - rows
    for rank in range(levels):
        at = (rank + level) % levels
        lay_block(lat_count, window, rows, store_of((1 - rank) * rows, at, side, False))
        first = levels * rows + (2 - rank) * height
        lay_rims(lat_count, window, rows, store_of(first, at, side, False))
    lay_rims(lat_count, window, rows, store_of(levels * rows, 1 - level, 1, True))
    for k in range(levels):
        for spot in spots:
            share = [rows_of(laid, k * kinds + kind, window, spot) for kind in range(kinds)]
            for size in range(bins):
                at = piece(k * bins + size, window, spot)
                coarse[at] = begun[at] + share[size]
            wind, wind_next, mask_share = share[bins:]
            stay, next_sweep, sweep = (
                begun[piece(fields + 3 * k + index, window, spot)] + value
                for index, value in enumerate((-wind, wind_next, wind))
            )
            last_sweep, over_sweep = pltpu.roll(sweep, LANES - 1, 1), pltpu.roll(next_sweep, 1, 1)
            kept = 1.0 - 3.0 * diffusion
            for index, value in enumerate(
                (kept - last_sweep, stay, kept - next_sweep, last_sweep, sweep, next_sweep, over_sweep)
            ):
                winds[piece(7 * k + index, window, spot)] = value
            if k == 0:
                winds[piece(7 * levels, window, spot)] = begun[piece(fields + 3 * levels, window, spot)] + mask_share

    sub = lax.broadcasted_iota(jnp.int32, (EDGE, LANES), 0)

    def copies(cells, reach):
        out = {0: cells}
        for turn in range(1, reach + 1):
            out[turn] = [pltpu.roll(value, turn, 1) for value in cells]
            out[-turn] = [pltpu.roll(value, LANES - turn, 1) for value in cells]
        return out

    def carried_at(turned, k, backward, turn):
        cells, west, east = turned[turn], turned[turn + 1], turned[turn - 1]
        out = []
        for spot in spots:
            if spot:
                south = cells[spot - 1]
            else:
                south = jnp.where(sub == 0, 0.0, pltpu.roll(cells[-1], 1, 0))
            if spot < count - 1:
                north = cells[spot + 1]
            else:
                north = jnp.where(sub == EDGE - 1, 0.0, pltpu.roll(cells[0], EDGE - 1, 0))
            swept, other = (east[spot], west[spot]) if backward else (west[spot], east[spot])
            near = diffusion * ((north + south) + other)
            sweep = 7 * k + 4 + turn + (not backward)
            out.append(
                (near + winds[piece(7 * k + 1 + turn, window, spot)] * cells[spot])
                + winds[piece(sweep, window, spot)] * swept
            )
        return out

    def carried(cells, k, backward):
        return carried_at(copies(cells, 1), k, backward, 0)

    def each(function, *lists):
        return [function(*values) for values in zip(*lists)]

    def added(first, second):
        return each(lambda a, b: a + b, first, second)

    def total_of(lists):
        out = lists[0]
        for values in lists[1:]:
            out = added(out, values)
        return out

    def scaled(factor, values):
        return [factor * value for value in values]

    def more(base, factor, values):
        return each(lambda a, b: a + factor * b, base, values)

    sizes = range(bins)
    upper = [scales[size, :1] for size in sizes]
    lower = [scales[bins + size, :1] for size in sizes]

    def summed_forward(top, bottom):
        sunk = [[] for _ in range(3)]
        cells = top
        for index in range(3):
            sunk[index] = [scaled(upper[size], cells[size]) for size in sizes]
            if index < 2:
                cells = [each(lambda a, b: a - b, carried(cells[size], 0, False), sunk[index][size]) for size in sizes]
        turned, sinking = copies(total_of(cells), 2), copies(total_of(sunk[2]), 1)
        both = {
            turn: each(lambda a, b: a - b, carried_at(turned, 0, False, turn), sinking[turn]) for turn in (-1, 0, 1)
        }
        both = carried_at(both, 0, False, 0)
        factors = []
        for size in sizes:
            rate = -lower[size]
            first = scaled(rate, bottom[size])
            b3 = added(sunk[0][size], first)
            b2 = more(sunk[1][size], rate, b3)
            b1 = more(sunk[2][size], rate, b2)
            c0 = scaled(rate, b1)
            e3 = added(b3, first)
            e2 = more(b2, rate, e3)
            c1 = more(b1, rate, e2)
            f3 = added(e3, first)
            c2 = more(e2, rate, f3)
            c3 = added(f3, first)
            factors.append([c3, c2, c1, c0])
        moved = total_of(bottom)
        sums = [total_of([factor[index] for factor in factors]) for index in range(4)]
        for index in range(2):
            moved = added(carried(moved, 1, False), sums[index])
        turned, third = copies(moved, 2), copies(sums[2], 1)
        moved = {turn: added(carried_at(turned, 1, False, turn), third[turn]) for turn in (-1, 0, 1)}
        return added(both, added(carried_at(moved, 1, False, 0), sums[3]))

    def spread_backward(start):
        turned = copies(start, 2)
        lower_one, upper_one = (
            {turn: carried_at(turned, k, True, turn) for turn in (-1, 0, 1)} for k in (1, 0)
        )
        powers = [start, lower_one[0], carried_at(lower_one, 1, True, 0)]
        for _ in range(2):
            powers.append(carried(powers[-1], 1, True))
        twice, thrice, thrice_more = scaled(2.0, powers[1]), scaled(3.0, powers[1]), scaled(3.0, powers[2])
        four, six, four_more = scaled(4.0, powers[1]), scaled(6.0, powers[2]), scaled(4.0, powers[3])
        first, second = upper_one[0], carried_at(upper_one, 0, True, 0)
        gap = each(lambda a, b: a - b, powers[1], first)
        tops, bottoms = [], []
        for size in sizes:
            rate = -lower[size]
            low_two = more(powers[2], rate, more(twice, rate, start))
            low_three = more(powers[3], rate, more(thrice_more, rate, more(thrice, rate, start)))
            low_four = more(powers[4], rate, more(four_more, rate, more(six, rate, more(four, rate, start))))
            cells = more(second, upper[size], more(gap, rate, start))
            for below in (low_two, low_three):
                cells = more(carried(cells, 0, True), upper[size], each(lambda a, b: a - b, below, cells))
            tops.append(cells)
            bottoms.append(low_four)
        return tops + bottoms

    scale = 1.0 / fields
    mask = [winds[piece(7 * levels, window, spot)] for spot in spots]
    for field in range(fields):
        for spot in spots:
            change[piece(field, window, spot)] = jnp.zeros((EDGE, LANES), jnp.float32)

    def one_sweep(sweep, carry):
        cells = [[coarse[piece(field, window, spot)] for spot in spots] for field in range(fields)]
        if True:
            cells = [added(cells[field], [change[piece(field, window, spot)] for spot in spots]) for field in range(fields)]
        total = summed_forward(cells[:bins], cells[bins:])
        start = [
            rows_of(table, 0, window, spot) * (total[spot] * (scale * scale)) - rows_of(table, 1, window, spot) * scale
            for spot in spots
        ]
        adjoint = spread_backward(start)
        for field in range(fields):
            for spot in spots:
                if True:
                    old = change[piece(field, window, spot)]
                    value = old - step_length * (background * old + adjoint[field][spot])
                else:
                    value = -step_length * adjoint[field][spot]
                change[piece(field, window, spot)] = mask[spot] * value
        return carry

    lax.fori_loop(0, SWEEPS, one_sweep, 0)

    for field in range(fields):
        for spot in spots:
            coarse[pl.ds(field * window + spot, EDGE, stride=count), :] = change[piece(field, window, spot)]
    final = [
        coarse[pl.ds(pl.multiple_of((level * bins + size) * window + own, 8), rows)] for size in range(bins)
    ]
    for size in range(bins):
        turned = final[size].T
        for slot in range(slots):
            start = slot * HALF + cols
            correction[slot, size, 0] = turned[start : start + cols]
    writes = [pltpu.make_async_copy(correction, correction_out, written.at[slots * bins])]
    writes[0].start()
    source_lane = lax.broadcasted_iota(jnp.int32, (LANES, slots * LANES), 0)
    target_lane = lax.broadcasted_iota(jnp.int32, (LANES, slots * LANES), 1)
    picks = source_lane == target_lane // LANES * HALF + cols + target_lane % LANES // BLOCK
    picks = picks.astype(jnp.float32).astype(jnp.bfloat16)
    wide = jnp.dot(
        three_parts(jnp.concatenate(final)), jnp.concatenate([picks] * 3), preferred_element_type=jnp.float32
    )
    growth = scales[levels * bins]
    fetch.wait()
    for slot in range(slots):
        for size in range(bins):
            cells = wide[size * rows : (size + 1) * rows, slot * LANES : (slot + 1) * LANES]
            raised = (cells[:, None, :] * growth[None]).reshape(rows * BLOCK, LANES)
            analysis[slot, size, 0] = (fine[slot, size, 0].astype(jnp.float32) + raised).astype(jnp.bfloat16)
            at = (slot, size)
            writes.append(pltpu.make_async_copy(analysis.at[at], analysis_out.at[at], written.at[slot * bins + size]))
            writes[-1].start()
    for write in writes:
        write.wait()


def solution(mesh):
    lon_count, lat_count, lev_count = (mesh.shape[axis] for axis in AXES)

    def place_of(lon, lat, lev):
        return (lon % lon_count * lat_count + lat) * lev_count + lev

    def moved(values, source_of):
        pairs = []
        for lon in range(lon_count):
            for lat in range(lat_count):
                for lev in range(lev_count):
                    source = source_of(lon, lat, lev)
                    if source is not None:
                        pairs.append((place_of(*source), place_of(lon, lat, lev)))
        return lax.ppermute(values, AXES, pairs)

    def per_device(
        trajectory,
        block_weights,
        wind_speed,
        settling,
        source_mask,
        obs_columns,
        obs_values,
        obs_weights,
    ):
        slots, bins, _, fine_rows, fine_cols = trajectory.shape
        rows, cols = fine_rows // BLOCK, fine_cols // BLOCK
        rims = min(lat_count - 1, 2)
        window = rows + rims * REACH
        small = pltpu.CompilerParams(vmem_limit_bytes=8 * 1024 * 1024)
        in_vmem = pl.BlockSpec(memory_space=pltpu.VMEM)

        def kept(array):
            return pltpu.with_memory_space_constraint(array, pltpu.HBM)

        in_hbm = pl.BlockSpec(memory_space=pltpu.HBM)

        def restrict(*refs):
            restrict_kernel(lat_count, slots, bins, rows, cols, *refs)

        packed = pl.pallas_call(
            restrict,
            out_shape=pltpu.VMEM((rows, LANES), jnp.float32),
            in_specs=[in_hbm] * 4,
            out_specs=in_vmem,
            scratch_shapes=[
                pltpu.VMEM(trajectory.shape, jnp.bfloat16),
                pltpu.VMEM((BLOCK, BLOCK), jnp.float32),
                pltpu.VMEM((1, cols, rows), jnp.float32),
                pltpu.VMEM((cols, rows), jnp.int32),
                pltpu.VMEM((slots * bins * fine_rows, LANES), jnp.float32),
                pltpu.SemaphoreType.DMA((3 + slots * bins,)),
            ],
            compiler_params=small,
        )(*map(kept, (trajectory, block_weights, wind_speed.swapaxes(1, 2), source_mask.T)))

        def tabulate(*refs):
            obs_kernel(lat_count, lon_count * cols, rows, cols, window, *refs)

        observed = (
            obs_columns.T,
            obs_values.swapaxes(1, 2),
            obs_weights.swapaxes(1, 2),
            settling.T,
            block_weights,
        )
        table, scales = pl.pallas_call(
            tabulate,
            out_shape=(
                pltpu.VMEM((2, window, LANES), jnp.float32),
                pltpu.VMEM((2 * bins + 1, BLOCK, LANES), jnp.float32),
            ),
            in_specs=[in_hbm] * 5,
            out_specs=(in_vmem, in_vmem),
            scratch_shapes=[pltpu.VMEM(array.shape, array.dtype) for array in observed]
            + [pltpu.SemaphoreType.DMA((5,))],
            compiler_params=small,
        )(*map(kept, observed))

        own = jnp.stack([packed, moved(packed, lambda lon, lat, lev: (lon, lat, 1 - lev))])
        near = moved(own, lambda lon, lat, lev: (lon ^ 1 if lev == 0 else lon + 1 - 2 * ((lon + 1) % 2), lat, lev))
        held = jnp.concatenate([packed[None], near])
        if lat_count == 2:
            rims = moved(held[:, :REACH], lambda lon, lat, lev: (lon, 1 - lat, lev))
        else:
            low = moved(
                held[:, rows - REACH :], lambda lon, lat, lev: (lon, lat - 1, lev) if lat > 0 else None
            )
            high = moved(
                held[:, :REACH], lambda lon, lat, lev: (lon, lat + 1, lev) if lat < lat_count - 1 else None
            )
            rims = jnp.concatenate([low, high], axis=1)
        rims, table, scales = lax.optimization_barrier((rims, table, scales))
        brought = jnp.concatenate([near.reshape(-1, LANES), rims.reshape(-1, LANES)])
        far = moved(brought, lambda lon, lat, lev: (lon, lat, 1 - lev))

        def cycle(*refs):
            cycle_kernel(lat_count, slots, bins, rows, cols, window, *refs)

        fields = 2 * bins
        fields = 2 * bins
        field_shape = ((fields + 7) * window, LANES)

        def unpack(*refs):
            unpack_kernel(lat_count, bins, rows, cols, window, *refs)

        begun = pl.pallas_call(
            unpack,
            out_shape=pltpu.VMEM(field_shape, jnp.float32),
            in_specs=[in_vmem] * 3,
            out_specs=in_vmem,
            scratch_shapes=[pltpu.VMEM((4 * window, LANES), jnp.float32)],
            compiler_params=small,
        )(own, near, rims)
        begun, far = lax.optimization_barrier((begun, far))
        field_store = pltpu.VMEM((fields * window, LANES), jnp.float32)
        analysis, correction = pl.pallas_call(
            cycle,
            out_shape=(
                jax.ShapeDtypeStruct(trajectory.shape, jnp.bfloat16),
                jax.ShapeDtypeStruct((slots, bins, 1, cols, rows), jnp.float32),
            ),
            in_specs=[in_vmem] * 4 + [in_hbm],
            out_specs=(in_hbm, in_hbm),
            scratch_shapes=[
                pltpu.VMEM(trajectory.shape, jnp.bfloat16),
                pltpu.VMEM(trajectory.shape, jnp.bfloat16),
                pltpu.VMEM((slots, bins, 1, cols, rows), jnp.float32),
                field_store,
                field_store,
                pltpu.VMEM((15 * window, LANES), jnp.float32),
                pltpu.VMEM((2 * (bins + 3) * window, LANES), jnp.float32),
                pltpu.SemaphoreType.DMA,
                pltpu.SemaphoreType.DMA((slots * bins + 1,)),
            ],
            compiler_params=small,
        )(begun, far, table.reshape(-1, LANES), scales, kept(trajectory))
        return analysis, correction.swapaxes(3, 4)

    placed = (
        P("member", None, "lev", "lat", "lon"),
        P(),
        P("lev", "lat", "lon"),
        P(),
        P("lat", "lon"),
        P("member", None),
        P("member", None, None),
        P("member", None, None),
    )
    return jax.shard_map(
        per_device,
        mesh=mesh,
        in_specs=placed,
        out_specs=(P("member", None, "lev", "lat", "lon"), P("member", None, "lev", "lat", "lon")),
        check_vma=False,
    )
```

```python
import jax
import jax.numpy as jnp
from jax import lax
from jax.experimental import pallas as pl
from jax.experimental.pallas import tpu as pltpu
from jax.sharding import PartitionSpec as P

BLOCK = 8
STEPS = 4
SWEEPS = 2
REACH = STEPS * 2 * SWEEPS
LANES = 128
HALF = LANES // 2
EDGE = 8

diffusion = 0.05
background = 0.1
step_length = 4.0
AXES = ("lon", "lat", "lev")


def lane_iota(rows):
    return lax.broadcasted_iota(jnp.int32, (rows, LANES), 1)


def three_parts(values):
    high = values.astype(jnp.bfloat16)
    rest = values - high.astype(jnp.float32)
    middle = rest.astype(jnp.bfloat16)
    low = (rest - middle.astype(jnp.float32)).astype(jnp.bfloat16)
    return jnp.concatenate([high, middle, low], axis=1)


def weight_rows(weights):
    return jnp.concatenate([weights] * (LANES // BLOCK), axis=1)


def fetches_of(sources, held, copied):
    return [
        pltpu.make_async_copy(source, target, copied.at[index])
        for index, (source, target) in enumerate(zip(sources, held))
    ]


def restrict_kernel(lat_count, slots, bins, rows, cols, *refs):
    sources, packed, held, fine, copied = refs[:4], refs[4], refs[5:9], refs[9], refs[10]
    trajectory, weights, wind, mask = held
    parts = [(slot, size) for slot in range(slots) for size in range(bins)]
    fetches = fetches_of(
        [*sources[1:], *(sources[0].at[at] for at in parts)],
        [*held[1:], *(trajectory.at[at] for at in parts)],
        copied,
    )
    for fetch in fetches:
        fetch.start()
    for fetch in fetches[:3]:
        fetch.wait()
    rows_of_weights = weight_rows(weights[...])
    row_sums = []
    for index, at in enumerate(parts):
        fetches[3 + index].wait()
        start = index * rows * BLOCK
        fine[start : start + rows * BLOCK] = trajectory[at].reshape(rows * BLOCK, LANES).astype(jnp.float32)
        total = fine[pl.ds(start, rows, stride=BLOCK), :] * rows_of_weights[:1]
        for row in range(1, BLOCK):
            total += fine[pl.ds(start + row, rows, stride=BLOCK), :] * rows_of_weights[row : row + 1]
        row_sums.append(total)
    row_sums = jnp.concatenate(row_sums)
    cell = lax.broadcasted_iota(jnp.int32, (LANES, LANES), 0) // BLOCK
    pool = (cell == lane_iota(LANES) % cols).astype(jnp.float32).astype(jnp.bfloat16)
    pooled = jnp.dot(three_parts(row_sums), jnp.concatenate([pool] * 3), preferred_element_type=jnp.float32)
    group = lane_iota(rows) // cols
    filler = jnp.zeros((bins * cols, rows), jnp.float32)
    out = jnp.concatenate([filler, wind[0], filler, mask[...].astype(jnp.float32)], axis=0).T
    for slot in range(slots):
        for size in range(bins):
            start = (slot * bins + size) * rows
            out = jnp.where(
                group == slot * (bins + 1) + size, pooled[start : start + rows], out
            )
    if lat_count == 2:
        start = pl.multiple_of(jnp.where(lax.axis_index("lat") == 0, rows - REACH, 0), 8)
        packed[pl.ds(start, REACH)] = out[:REACH]
        packed[pl.ds(pl.multiple_of(rows - REACH - start, 8), REACH)] = out[REACH:]
    else:
        packed[...] = out


def window_start(lat_count, rows, window):
    lat = lax.axis_index("lat")
    own = jnp.where(lat == 0, 0, jnp.where(lat == lat_count - 1, window - rows, REACH))
    return lat, own


def obs_kernel(lat_count, lon_total, rows, cols, window, *refs):
    sources, (table, scales), held, copied = refs[:5], refs[5:7], refs[7:12], refs[12]
    fetches = fetches_of(sources, held, copied)
    for fetch in fetches:
        fetch.start()
    for fetch in fetches:
        fetch.wait()
    columns, values, obs_weights, settling, weights = held
    lat, own = window_start(lat_count, rows, window)
    first = lat * rows - own
    slots, obs, lat_total = values.shape
    wide = -(-lat_total // LANES) * LANES
    low = lane_iota(obs) < HALF

    def windowed(array):
        if wide > lat_total:
            array = jnp.concatenate([array, jnp.zeros((obs, wide - lat_total), array.dtype)], axis=1)
        return pltpu.roll(array, lax.rem(wide - first, wide), 1)[:, :LANES]

    def paired(first_slot, second_slot):
        return jnp.where(low, windowed(first_slot), pltpu.roll(windowed(second_slot), HALF, 1))

    held = columns[...].astype(jnp.float32)
    place = paired(held, held)
    weight = paired(obs_weights[0], obs_weights[1])
    product = paired(obs_weights[0] * values[0], obs_weights[1] * values[1])
    sub = lax.broadcasted_iota(jnp.int32, (HALF, LANES), 0)
    start = lax.axis_index("lon") * cols - cols + lon_total
    here = lax.rem(sub + start, lon_total).astype(jnp.float32)
    sum_weight = jnp.zeros((HALF, LANES), jnp.float32)
    sum_product = jnp.zeros((HALF, LANES), jnp.float32)
    for index in range(obs):
        hit = here == place[index : index + 1]
        sum_weight += jnp.where(hit, weight[index : index + 1], 0.0)
        sum_product += jnp.where(hit, product[index : index + 1], 0.0)
    both = jnp.concatenate([sum_weight, sum_product], axis=0).T
    left, right = both[:window], both[HALF : HALF + window]
    low = lane_iota(window) < HALF
    table[0] = jnp.where(low, left, pltpu.roll(right, HALF, 1))
    table[1] = jnp.where(low, pltpu.roll(left, HALF, 1), right)
    levels, bins = settling.shape
    for k in range(levels):
        for size in range(bins):
            rate = settling[k : k + 1, size : size + 1]
            scales[k * bins + size] = jnp.broadcast_to(rate, (BLOCK, LANES))
    scales[levels * bins] = (BLOCK * BLOCK) * weight_rows(weights[...])


def rows_of(ref, field, window, spot):
    return ref[pl.ds(field * window + spot, EDGE, stride=window // EDGE), :]


def piece(field, window, spot):
    start = field * window + spot * EDGE
    return slice(start, start + EDGE)


def lay_block(lat_count, window, rows, store):
    lat, own = window_start(lat_count, rows, window)
    if lat_count == 2:
        store(0, REACH, REACH)
        store(REACH, rows - REACH, lat * 2 * REACH)
    else:
        store(0, rows, own)


def lay_rims(lat_count, window, rows, store):
    lat, own = window_start(lat_count, rows, window)
    if lat_count == 2:
        store(0, REACH, 2 * REACH - lat * 2 * REACH)
    else:
        pl.when(lat > 0)(lambda: store(0, REACH, own - REACH))
        pl.when(lat < lat_count - 1)(lambda: store(REACH, REACH, own + rows))


def near_is_west():
    return lax.rem(lax.axis_index("lon") + lax.axis_index("lev"), 2) == 1


def shares(block, place, bins, cols):
    lane = lane_iota(EDGE)
    low = lane < HALF
    zero = jnp.zeros((EDGE, LANES), jnp.float32)

    def turned(turn):
        return pltpu.roll(block, lax.rem(turn + 2 * LANES, LANES), 1)

    def inside(shift):
        from_start = lane - shift - place * cols
        return (from_start & (HALF - 1)) < cols

    out = [jnp.where(inside(0), turned((place - size) * cols), zero) for size in range(bins)]
    turn = (place - bins) * cols
    straight, crossed = turned(turn), turned(turn + HALF)
    out.append(jnp.where(inside(0), jnp.where(low, straight, crossed), zero))
    next_low = lax.rem(lane + LANES - 1, LANES) < HALF
    out.append(jnp.where(inside(1), jnp.where(next_low, turned(turn + 1), turned(turn + HALF + 1)), zero))
    out.append(jnp.where(inside(0), jnp.where(low, crossed, straight), zero))
    return out


def unpack_kernel(lat_count, bins, rows, cols, window, own_cells, near_cells, rims, begun, laid):
    levels = 2
    fields = levels * bins
    level = lax.axis_index("lev")
    laid[...] = jnp.zeros(laid.shape, jnp.float32)
    for rank in range(levels):
        at = (rank + level) % levels

        def store_of(block, place):
            def store(start, size, row):
                laid[pl.ds(pl.multiple_of(place * window + row, 8), size)] = block[pl.ds(start, size)]

            return store

        lay_block(lat_count, window, rows, store_of(own_cells.at[rank], at * 2))
        lay_block(lat_count, window, rows, store_of(near_cells.at[rank], at * 2 + 1))
        if rank == 0:
            lay_rims(lat_count, window, rows, store_of(rims.at[0], at * 2))
        lay_rims(lat_count, window, rows, store_of(rims.at[1 + rank], at * 2 + 1))
    side = jnp.where(near_is_west(), 0, 2)
    for k in range(levels):
        for spot in range(window // EDGE):
            center = shares(rows_of(laid, 2 * k, window, spot), 1, bins, cols)
            beside = shares(rows_of(laid, 2 * k + 1, window, spot), side, bins, cols)
            both = [a + b for a, b in zip(center, beside)]
            for size in range(bins):
                begun[piece(k * bins + size, window, spot)] = both[size]
            wind, wind_next, mask = both[bins:]
            begun[piece(fields + 3 * k, window, spot)] = 1.0 - 4.0 * diffusion - wind
            begun[piece(fields + 3 * k + 1, window, spot)] = wind_next + diffusion
            begun[piece(fields + 3 * k + 2, window, spot)] = wind + diffusion
            if k == 0:
                begun[piece(fields + 3 * levels, window, spot)] = mask


def cycle_kernel(
    lat_count,
    slots,
    bins,
    rows,
    cols,
    window,
    begun,
    far,
    table,
    scales,
    trajectory,
    analysis_out,
    correction_out,
    fine,
    analysis,
    correction,
    coarse,
    change,
    winds,
    laid,
    copied,
    written,
):
    fetch = pltpu.make_async_copy(trajectory, fine, copied)
    fetch.start()
    levels = 2
    fields = levels * bins
    lat, own = window_start(lat_count, rows, window)
    level = lax.axis_index("lev")
    count = window // EDGE
    spots = range(count)
    kinds = bins + 3
    side = jnp.where(near_is_west(), 2, 0)
    if lat_count != 2:
        laid[...] = jnp.zeros(laid.shape, jnp.float32)

    def store_of(first, at, place, more_to):
        def store(start, size, row):
            for part in range(0, size, EDGE):
                share = shares(far[pl.ds(first + start + part, EDGE)], place, bins, cols)
                for kind in range(kinds):
                    target = (at * kinds + kind) * window + row + part
                    target = pl.ds(pl.multiple_of(target, 8), EDGE)
                    laid[target] = laid[target] + share[kind] if more_to else share[kind]

        return store

    height = window - rows
    for rank in range(levels):
        at = (rank + level) % levels
        lay_block(lat_count, window, rows, store_of((1 - rank) * rows, at, side, False))
        first = levels * rows + (2 - rank) * height
        lay_rims(lat_count, window, rows, store_of(first, at, side, False))
    lay_rims(lat_count, window, rows, store_of(levels * rows, 1 - level, 1, True))
    for k in range(levels):
        for spot in spots:
            share = [rows_of(laid, k * kinds + kind, window, spot) for kind in range(kinds)]
            for size in range(bins):
                at = piece(k * bins + size, window, spot)
                coarse[at] = begun[at] + share[size]
            wind, wind_next, mask_share = share[bins:]
            stay, next_sweep, sweep = (
                begun[piece(fields + 3 * k + index, window, spot)] + value
                for index, value in enumerate((-wind, wind_next, wind))
            )
            last_sweep, over_sweep = pltpu.roll(sweep, LANES - 1, 1), pltpu.roll(next_sweep, 1, 1)
            kept = 1.0 - 3.0 * diffusion
            for index, value in enumerate(
                (kept - last_sweep, stay, kept - next_sweep, last_sweep, sweep, next_sweep, over_sweep)
            ):
                winds[piece(7 * k + index, window, spot)] = value
            if k == 0:
                winds[piece(7 * levels, window, spot)] = begun[piece(fields + 3 * levels, window, spot)] + mask_share

    sub = lax.broadcasted_iota(jnp.int32, (EDGE, LANES), 0)

    def copies(cells, reach):
        out = {0: cells}
        for turn in range(1, reach + 1):
            out[turn] = [pltpu.roll(value, turn, 1) for value in cells]
            out[-turn] = [pltpu.roll(value, LANES - turn, 1) for value in cells]
        return out

    def carried_at(turned, k, backward, turn):
        cells, west, east = turned[turn], turned[turn + 1], turned[turn - 1]
        out = []
        for spot in spots:
            if spot:
                south = cells[spot - 1]
            else:
                south = jnp.where(sub == 0, 0.0, pltpu.roll(cells[-1], 1, 0))
            if spot < count - 1:
                north = cells[spot + 1]
            else:
                north = jnp.where(sub == EDGE - 1, 0.0, pltpu.roll(cells[0], EDGE - 1, 0))
            swept, other = (east[spot], west[spot]) if backward else (west[spot], east[spot])
            near = diffusion * ((north + south) + other)
            sweep = 7 * k + 4 + turn + (not backward)
            out.append(
                (near + winds[piece(7 * k + 1 + turn, window, spot)] * cells[spot])
                + winds[piece(sweep, window, spot)] * swept
            )
        return out

    def carried(cells, k, backward):
        return carried_at(copies(cells, 1), k, backward, 0)

    def each(function, *lists):
        return [function(*values) for values in zip(*lists)]

    def added(first, second):
        return each(lambda a, b: a + b, first, second)

    def total_of(lists):
        out = lists[0]
        for values in lists[1:]:
            out = added(out, values)
        return out

    def scaled(factor, values):
        return [factor * value for value in values]

    def more(base, factor, values):
        return each(lambda a, b: a + factor * b, base, values)

    sizes = range(bins)
    upper = [scales[size, :1] for size in sizes]
    lower = [scales[bins + size, :1] for size in sizes]

    def summed_forward(top, bottom):
        sunk = [[] for _ in range(3)]
        cells = top
        for index in range(3):
            sunk[index] = [scaled(upper[size], cells[size]) for size in sizes]
            if index < 2:
                cells = [each(lambda a, b: a - b, carried(cells[size], 0, False), sunk[index][size]) for size in sizes]
        turned, sinking = copies(total_of(cells), 2), copies(total_of(sunk[2]), 1)
        both = {
            turn: each(lambda a, b: a - b, carried_at(turned, 0, False, turn), sinking[turn]) for turn in (-1, 0, 1)
        }
        both = carried_at(both, 0, False, 0)
        factors = []
        for size in sizes:
            rate = -lower[size]
            first = scaled(rate, bottom[size])
            b3 = added(sunk[0][size], first)
            b2 = more(sunk[1][size], rate, b3)
            b1 = more(sunk[2][size], rate, b2)
            c0 = scaled(rate, b1)
            e3 = added(b3, first)
            e2 = more(b2, rate, e3)
            c1 = more(b1, rate, e2)
            f3 = added(e3, first)
            c2 = more(e2, rate, f3)
            c3 = added(f3, first)
            factors.append([c3, c2, c1, c0])
        moved = total_of(bottom)
        sums = [total_of([factor[index] for factor in factors]) for index in range(4)]
        for index in range(2):
            moved = added(carried(moved, 1, False), sums[index])
        turned, third = copies(moved, 2), copies(sums[2], 1)
        moved = {turn: added(carried_at(turned, 1, False, turn), third[turn]) for turn in (-1, 0, 1)}
        return added(both, added(carried_at(moved, 1, False, 0), sums[3]))

    def spread_backward(start):
        turned = copies(start, 2)
        lower_one, upper_one = (
            {turn: carried_at(turned, k, True, turn) for turn in (-1, 0, 1)} for k in (1, 0)
        )
        powers = [start, lower_one[0], carried_at(lower_one, 1, True, 0)]
        later = copies(powers[2], 2)
        lower_three = {turn: carried_at(later, 1, True, turn) for turn in (-1, 0, 1)}
        powers += [lower_three[0], carried_at(lower_three, 1, True, 0)]
        twice, thrice, thrice_more = scaled(2.0, powers[1]), scaled(3.0, powers[1]), scaled(3.0, powers[2])
        four, six, four_more = scaled(4.0, powers[1]), scaled(6.0, powers[2]), scaled(4.0, powers[3])
        first, second = upper_one[0], carried_at(upper_one, 0, True, 0)
        gap = each(lambda a, b: a - b, powers[1], first)
        third = carried(second, 0, True)
        next_gap = each(lambda a, b: a - b, carried_at(lower_one, 0, True, 0), second)
        tops, bottoms = [], []
        for size in sizes:
            rate = -lower[size]
            low_two = more(powers[2], rate, more(twice, rate, start))
            low_three = more(powers[3], rate, more(thrice_more, rate, more(thrice, rate, start)))
            low_four = more(powers[4], rate, more(four_more, rate, more(six, rate, more(four, rate, start))))
            cells = more(second, upper[size], more(gap, rate, start))
            gain = added(more(next_gap, rate, first), each(lambda a, b: a - b, low_two, cells))
            cells = more(third, upper[size], gain)
            gain = each(lambda a, b: a - b, low_three, cells)
            cells = more(carried(cells, 0, True), upper[size], gain)
            tops.append(cells)
            bottoms.append(low_four)
        return tops + bottoms

    scale = 1.0 / fields
    mask = [winds[piece(7 * levels, window, spot)] for spot in spots]
    for sweep in range(SWEEPS):
        cells = [[coarse[piece(field, window, spot)] for spot in spots] for field in range(fields)]
        if sweep:
            cells = [added(cells[field], [change[piece(field, window, spot)] for spot in spots]) for field in range(fields)]
        total = summed_forward(cells[:bins], cells[bins:])
        start = [
            rows_of(table, 0, window, spot) * (total[spot] * (scale * scale)) - rows_of(table, 1, window, spot) * scale
            for spot in spots
        ]
        adjoint = spread_backward(start)
        for field in range(fields):
            for spot in spots:
                if sweep:
                    old = change[piece(field, window, spot)]
                    value = old - step_length * (background * old + adjoint[field][spot])
                else:
                    value = -step_length * adjoint[field][spot]
                if sweep < SWEEPS - 1:
                    change[piece(field, window, spot)] = mask[spot] * value
                else:
                    coarse[pl.ds(field * window + spot, EDGE, stride=count), :] = mask[spot] * value

    final = [
        coarse[pl.ds(pl.multiple_of((level * bins + size) * window + own, 8), rows)] for size in range(bins)
    ]
    for size in range(bins):
        turned = final[size].T
        for slot in range(slots):
            start = slot * HALF + cols
            correction[slot, size, 0] = turned[start : start + cols]
    writes = [pltpu.make_async_copy(correction, correction_out, written.at[slots * bins])]
    writes[0].start()
    source_lane = lax.broadcasted_iota(jnp.int32, (LANES, slots * LANES), 0)
    target_lane = lax.broadcasted_iota(jnp.int32, (LANES, slots * LANES), 1)
    picks = source_lane == target_lane // LANES * HALF + cols + target_lane % LANES // BLOCK
    picks = picks.astype(jnp.float32).astype(jnp.bfloat16)
    wide = jnp.dot(
        three_parts(jnp.concatenate(final)), jnp.concatenate([picks] * 3), preferred_element_type=jnp.float32
    )
    growth = scales[levels * bins]
    fetch.wait()
    for slot in range(slots):
        for size in range(bins):
            cells = wide[size * rows : (size + 1) * rows, slot * LANES : (slot + 1) * LANES]
            raised = (cells[:, None, :] * growth[None]).reshape(rows * BLOCK, LANES)
            analysis[slot, size, 0] = (fine[slot, size, 0].astype(jnp.float32) + raised).astype(jnp.bfloat16)
            at = (slot, size)
            writes.append(pltpu.make_async_copy(analysis.at[at], analysis_out.at[at], written.at[slot * bins + size]))
            writes[-1].start()
    for write in writes:
        write.wait()


def solution(mesh):
    lon_count, lat_count, lev_count = (mesh.shape[axis] for axis in AXES)

    def place_of(lon, lat, lev):
        return (lon % lon_count * lat_count + lat) * lev_count + lev

    def moved(values, source_of):
        pairs = []
        for lon in range(lon_count):
            for lat in range(lat_count):
                for lev in range(lev_count):
                    source = source_of(lon, lat, lev)
                    if source is not None:
                        pairs.append((place_of(*source), place_of(lon, lat, lev)))
        return lax.ppermute(values, AXES, pairs)

    def per_device(
        trajectory,
        block_weights,
        wind_speed,
        settling,
        source_mask,
        obs_columns,
        obs_values,
        obs_weights,
    ):
        slots, bins, _, fine_rows, fine_cols = trajectory.shape
        rows, cols = fine_rows // BLOCK, fine_cols // BLOCK
        rims = min(lat_count - 1, 2)
        window = rows + rims * REACH
        small = pltpu.CompilerParams(vmem_limit_bytes=8 * 1024 * 1024)
        in_vmem = pl.BlockSpec(memory_space=pltpu.VMEM)

        def kept(array):
            return pltpu.with_memory_space_constraint(array, pltpu.HBM)

        in_hbm = pl.BlockSpec(memory_space=pltpu.HBM)

        def restrict(*refs):
            restrict_kernel(lat_count, slots, bins, rows, cols, *refs)

        packed = pl.pallas_call(
            restrict,
            out_shape=pltpu.VMEM((rows, LANES), jnp.float32),
            in_specs=[in_hbm] * 4,
            out_specs=in_vmem,
            scratch_shapes=[
                pltpu.VMEM(trajectory.shape, jnp.bfloat16),
                pltpu.VMEM((BLOCK, BLOCK), jnp.float32),
                pltpu.VMEM((1, cols, rows), jnp.float32),
                pltpu.VMEM((cols, rows), jnp.int32),
                pltpu.VMEM((slots * bins * fine_rows, LANES), jnp.float32),
                pltpu.SemaphoreType.DMA((3 + slots * bins,)),
            ],
            compiler_params=small,
        )(*map(kept, (trajectory, block_weights, wind_speed.swapaxes(1, 2), source_mask.T)))

        def tabulate(*refs):
            obs_kernel(lat_count, lon_count * cols, rows, cols, window, *refs)

        observed = (
            obs_columns.T,
            obs_values.swapaxes(1, 2),
            obs_weights.swapaxes(1, 2),
            settling.T,
            block_weights,
        )
        table, scales = pl.pallas_call(
            tabulate,
            out_shape=(
                pltpu.VMEM((2, window, LANES), jnp.float32),
                pltpu.VMEM((2 * bins + 1, BLOCK, LANES), jnp.float32),
            ),
            in_specs=[in_hbm] * 5,
            out_specs=(in_vmem, in_vmem),
            scratch_shapes=[pltpu.VMEM(array.shape, array.dtype) for array in observed]
            + [pltpu.SemaphoreType.DMA((5,))],
            compiler_params=small,
        )(*map(kept, observed))

        own = jnp.stack([packed, moved(packed, lambda lon, lat, lev: (lon, lat, 1 - lev))])
        near = moved(own, lambda lon, lat, lev: (lon ^ 1 if lev == 0 else lon + 1 - 2 * ((lon + 1) % 2), lat, lev))
        held = jnp.concatenate([packed[None], near])
        if lat_count == 2:
            rims = moved(held[:, :REACH], lambda lon, lat, lev: (lon, 1 - lat, lev))
        else:
            low = moved(
                held[:, rows - REACH :], lambda lon, lat, lev: (lon, lat - 1, lev) if lat > 0 else None
            )
            high = moved(
                held[:, :REACH], lambda lon, lat, lev: (lon, lat + 1, lev) if lat < lat_count - 1 else None
            )
            rims = jnp.concatenate([low, high], axis=1)
        rims, table, scales = lax.optimization_barrier((rims, table, scales))
        brought = jnp.concatenate([near.reshape(-1, LANES), rims.reshape(-1, LANES)])
        far = moved(brought, lambda lon, lat, lev: (lon, lat, 1 - lev))

        def cycle(*refs):
            cycle_kernel(lat_count, slots, bins, rows, cols, window, *refs)

        fields = 2 * bins
        fields = 2 * bins
        field_shape = ((fields + 7) * window, LANES)

        def unpack(*refs):
            unpack_kernel(lat_count, bins, rows, cols, window, *refs)

        begun = pl.pallas_call(
            unpack,
            out_shape=pltpu.VMEM(field_shape, jnp.float32),
            in_specs=[in_vmem] * 3,
            out_specs=in_vmem,
            scratch_shapes=[pltpu.VMEM((4 * window, LANES), jnp.float32)],
            compiler_params=small,
        )(own, near, rims)
        begun, far = lax.optimization_barrier((begun, far))
        field_store = pltpu.VMEM((fields * window, LANES), jnp.float32)
        analysis, correction = pl.pallas_call(
            cycle,
            out_shape=(
                jax.ShapeDtypeStruct(trajectory.shape, jnp.bfloat16),
                jax.ShapeDtypeStruct((slots, bins, 1, cols, rows), jnp.float32),
            ),
            in_specs=[in_vmem] * 4 + [in_hbm],
            out_specs=(in_hbm, in_hbm),
            scratch_shapes=[
                pltpu.VMEM(trajectory.shape, jnp.bfloat16),
                pltpu.VMEM(trajectory.shape, jnp.bfloat16),
                pltpu.VMEM((slots, bins, 1, cols, rows), jnp.float32),
                field_store,
                field_store,
                pltpu.VMEM((15 * window, LANES), jnp.float32),
                pltpu.VMEM((2 * (bins + 3) * window, LANES), jnp.float32),
                pltpu.SemaphoreType.DMA,
                pltpu.SemaphoreType.DMA((slots * bins + 1,)),
            ],
            compiler_params=small,
        )(begun, far, table.reshape(-1, LANES), scales, kept(trajectory))
        return analysis, correction.swapaxes(3, 4)

    placed = (
        P("member", None, "lev", "lat", "lon"),
        P(),
        P("lev", "lat", "lon"),
        P(),
        P("lat", "lon"),
        P("member", None),
        P("member", None, None),
        P("member", None, None),
    )
    return jax.shard_map(
        per_device,
        mesh=mesh,
        in_specs=placed,
        out_specs=(P("member", None, "lev", "lat", "lon"), P("member", None, "lev", "lat", "lon")),
        check_vma=False,
    )
```

```python
import jax
import jax.numpy as jnp
from jax import lax
from jax.experimental import pallas as pl
from jax.experimental.pallas import tpu as pltpu
from jax.sharding import PartitionSpec as P

BLOCK = 8
STEPS = 4
SWEEPS = 2
REACH = STEPS * 2 * SWEEPS
LANES = 128
HALF = LANES // 2
EDGE = 8

diffusion = 0.05
background = 0.1
step_length = 4.0
AXES = ("lon", "lat", "lev")


def lane_iota(rows):
    return lax.broadcasted_iota(jnp.int32, (rows, LANES), 1)


def three_parts(values):
    high = values.astype(jnp.bfloat16)
    rest = values - high.astype(jnp.float32)
    middle = rest.astype(jnp.bfloat16)
    low = (rest - middle.astype(jnp.float32)).astype(jnp.bfloat16)
    return jnp.concatenate([high, middle, low], axis=1)


def weight_rows(weights):
    return jnp.concatenate([weights] * (LANES // BLOCK), axis=1)


def fetches_of(sources, held, copied):
    return [
        pltpu.make_async_copy(source, target, copied.at[index])
        for index, (source, target) in enumerate(zip(sources, held))
    ]


def restrict_kernel(lat_count, slots, bins, rows, cols, *refs):
    sources, packed, held, fine, copied = refs[:4], refs[4], refs[5:9], refs[9], refs[10]
    trajectory, weights, wind, mask = held
    parts = [(slot, size) for slot in range(slots) for size in range(bins)]
    fetches = fetches_of(
        [*sources[1:], *(sources[0].at[at] for at in parts)],
        [*held[1:], *(trajectory.at[at] for at in parts)],
        copied,
    )
    for fetch in fetches:
        fetch.start()
    for fetch in fetches[:3]:
        fetch.wait()
    rows_of_weights = weight_rows(weights[...])
    row_sums = []
    for index, at in enumerate(parts):
        fetches[3 + index].wait()
        start = index * rows * BLOCK
        fine[start : start + rows * BLOCK] = trajectory[at].reshape(rows * BLOCK, LANES).astype(jnp.float32)
        total = fine[pl.ds(start, rows, stride=BLOCK), :] * rows_of_weights[:1]
        for row in range(1, BLOCK):
            total += fine[pl.ds(start + row, rows, stride=BLOCK), :] * rows_of_weights[row : row + 1]
        row_sums.append(total)
    row_sums = jnp.concatenate(row_sums)
    cell = lax.broadcasted_iota(jnp.int32, (LANES, LANES), 0) // BLOCK
    pool = (cell == lane_iota(LANES) % cols).astype(jnp.float32).astype(jnp.bfloat16)
    pooled = jnp.dot(three_parts(row_sums), jnp.concatenate([pool] * 3), preferred_element_type=jnp.float32)
    group = lane_iota(rows) // cols
    filler = jnp.zeros((bins * cols, rows), jnp.float32)
    out = jnp.concatenate([filler, wind[0], filler, mask[...].astype(jnp.float32)], axis=0).T
    for slot in range(slots):
        for size in range(bins):
            start = (slot * bins + size) * rows
            out = jnp.where(
                group == slot * (bins + 1) + size, pooled[start : start + rows], out
            )
    if lat_count == 2:
        start = pl.multiple_of(jnp.where(lax.axis_index("lat") == 0, rows - REACH, 0), 8)
        packed[pl.ds(start, REACH)] = out[:REACH]
        packed[pl.ds(pl.multiple_of(rows - REACH - start, 8), REACH)] = out[REACH:]
    else:
        packed[...] = out


def window_start(lat_count, rows, window):
    lat = lax.axis_index("lat")
    own = jnp.where(lat == 0, 0, jnp.where(lat == lat_count - 1, window - rows, REACH))
    return lat, own


def obs_kernel(lat_count, lon_total, rows, cols, window, *refs):
    sources, (table, scales), held, copied = refs[:5], refs[5:7], refs[7:12], refs[12]
    fetches = fetches_of(sources, held, copied)
    for fetch in fetches:
        fetch.start()
    for fetch in fetches:
        fetch.wait()
    columns, values, obs_weights, settling, weights = held
    lat, own = window_start(lat_count, rows, window)
    first = lat * rows - own
    slots, obs, lat_total = values.shape
    wide = -(-lat_total // LANES) * LANES
    low = lane_iota(obs) < HALF

    def windowed(array):
        if wide > lat_total:
            array = jnp.concatenate([array, jnp.zeros((obs, wide - lat_total), array.dtype)], axis=1)
        return pltpu.roll(array, lax.rem(wide - first, wide), 1)[:, :LANES]

    def paired(first_slot, second_slot):
        return jnp.where(low, windowed(first_slot), pltpu.roll(windowed(second_slot), HALF, 1))

    held = columns[...].astype(jnp.float32)
    place = paired(held, held)
    weight = paired(obs_weights[0], obs_weights[1])
    product = paired(obs_weights[0] * values[0], obs_weights[1] * values[1])
    sub = lax.broadcasted_iota(jnp.int32, (HALF, LANES), 0)
    start = lax.axis_index("lon") * cols - cols + lon_total
    here = lax.rem(sub + start, lon_total).astype(jnp.float32)
    sum_weight = jnp.zeros((HALF, LANES), jnp.float32)
    sum_product = jnp.zeros((HALF, LANES), jnp.float32)
    for index in range(obs):
        hit = here == place[index : index + 1]
        sum_weight += jnp.where(hit, weight[index : index + 1], 0.0)
        sum_product += jnp.where(hit, product[index : index + 1], 0.0)
    both = jnp.concatenate([sum_weight, sum_product], axis=0).T
    left, right = both[:window], both[HALF : HALF + window]
    low = lane_iota(window) < HALF
    table[0] = jnp.where(low, left, pltpu.roll(right, HALF, 1))
    table[1] = jnp.where(low, pltpu.roll(left, HALF, 1), right)
    levels, bins = settling.shape
    for k in range(levels):
        for size in range(bins):
            rate = settling[k : k + 1, size : size + 1]
            scales[k * bins + size] = jnp.broadcast_to(rate, (BLOCK, LANES))
    scales[levels * bins] = (BLOCK * BLOCK) * weight_rows(weights[...])


def rows_of(ref, field, window, spot):
    return ref[pl.ds(field * window + spot, EDGE, stride=window // EDGE), :]


def piece(field, window, spot):
    start = field * window + spot * EDGE
    return slice(start, start + EDGE)


def lay_block(lat_count, window, rows, store):
    lat, own = window_start(lat_count, rows, window)
    if lat_count == 2:
        store(0, REACH, REACH)
        store(REACH, rows - REACH, lat * 2 * REACH)
    else:
        store(0, rows, own)


def lay_rims(lat_count, window, rows, store):
    lat, own = window_start(lat_count, rows, window)
    if lat_count == 2:
        store(0, REACH, 2 * REACH - lat * 2 * REACH)
    else:
        pl.when(lat > 0)(lambda: store(0, REACH, own - REACH))
        pl.when(lat < lat_count - 1)(lambda: store(REACH, REACH, own + rows))


def near_is_west():
    return lax.rem(lax.axis_index("lon") + lax.axis_index("lev"), 2) == 1


def shares(block, place, bins, cols):
    lane = lane_iota(EDGE)
    low = lane < HALF
    zero = jnp.zeros((EDGE, LANES), jnp.float32)

    def turned(turn):
        return pltpu.roll(block, lax.rem(turn + 2 * LANES, LANES), 1)

    def inside(shift):
        from_start = lane - shift - place * cols
        return (from_start & (HALF - 1)) < cols

    out = [jnp.where(inside(0), turned((place - size) * cols), zero) for size in range(bins)]
    turn = (place - bins) * cols
    straight, crossed = turned(turn), turned(turn + HALF)
    out.append(jnp.where(inside(0), jnp.where(low, straight, crossed), zero))
    next_low = lax.rem(lane + LANES - 1, LANES) < HALF
    out.append(jnp.where(inside(1), jnp.where(next_low, turned(turn + 1), turned(turn + HALF + 1)), zero))
    out.append(jnp.where(inside(0), jnp.where(low, crossed, straight), zero))
    return out


def unpack_kernel(lat_count, bins, rows, cols, window, own_cells, near_cells, own_rims, near_rims, begun, laid):
    levels = 2
    fields = levels * bins
    level = lax.axis_index("lev")
    laid[...] = jnp.zeros(laid.shape, jnp.float32)
    for rank in range(levels):
        at = (rank + level) % levels

        def store_of(block, place):
            def store(start, size, row):
                laid[pl.ds(pl.multiple_of(place * window + row, 8), size)] = block[pl.ds(start, size)]

            return store

        lay_block(lat_count, window, rows, store_of(own_cells.at[rank], at * 2))
        lay_block(lat_count, window, rows, store_of(near_cells.at[rank], at * 2 + 1))
        lay_rims(lat_count, window, rows, store_of(own_rims.at[rank], at * 2))
        lay_rims(lat_count, window, rows, store_of(near_rims.at[rank], at * 2 + 1))
    side = jnp.where(near_is_west(), 0, 2)
    for k in range(levels):
        for spot in range(window // EDGE):
            center = shares(rows_of(laid, 2 * k, window, spot), 1, bins, cols)
            beside = shares(rows_of(laid, 2 * k + 1, window, spot), side, bins, cols)
            both = [a + b for a, b in zip(center, beside)]
            for size in range(bins):
                begun[piece(k * bins + size, window, spot)] = both[size]
            wind, wind_next, mask = both[bins:]
            begun[piece(fields + 3 * k, window, spot)] = 1.0 - 4.0 * diffusion - wind
            begun[piece(fields + 3 * k + 1, window, spot)] = wind_next + diffusion
            begun[piece(fields + 3 * k + 2, window, spot)] = wind + diffusion
            if k == 0:
                begun[piece(fields + 3 * levels, window, spot)] = mask


def cycle_kernel(
    lat_count,
    slots,
    bins,
    rows,
    cols,
    window,
    begun,
    far,
    table,
    scales,
    trajectory,
    analysis_out,
    correction_out,
    fine,
    analysis,
    correction,
    coarse,
    change,
    winds,
    laid,
    copied,
    written,
):
    fetch = pltpu.make_async_copy(trajectory, fine, copied)
    fetch.start()
    levels = 2
    fields = levels * bins
    lat, own = window_start(lat_count, rows, window)
    level = lax.axis_index("lev")
    count = window // EDGE
    spots = range(count)
    kinds = bins + 3
    side = jnp.where(near_is_west(), 2, 0)
    if lat_count != 2:
        laid[...] = jnp.zeros(laid.shape, jnp.float32)

    def store_of(first, at):
        def store(start, size, row):
            for part in range(0, size, EDGE):
                share = shares(far[pl.ds(first + start + part, EDGE)], side, bins, cols)
                for kind in range(kinds):
                    target = (at * kinds + kind) * window + row + part
                    laid[pl.ds(pl.multiple_of(target, 8), EDGE)] = share[kind]

        return store

    height = window - rows
    for rank in range(levels):
        at = (rank + level) % levels
        lay_block(lat_count, window, rows, store_of((1 - rank) * rows, at))
        lay_rims(lat_count, window, rows, store_of(levels * rows + (1 - rank) * height, at))
    for k in range(levels):
        for spot in spots:
            share = [rows_of(laid, k * kinds + kind, window, spot) for kind in range(kinds)]
            for size in range(bins):
                at = piece(k * bins + size, window, spot)
                coarse[at] = begun[at] + share[size]
            wind, wind_next, mask_share = share[bins:]
            stay, next_sweep, sweep = (
                begun[piece(fields + 3 * k + index, window, spot)] + value
                for index, value in enumerate((-wind, wind_next, wind))
            )
            last_sweep, over_sweep = pltpu.roll(sweep, LANES - 1, 1), pltpu.roll(next_sweep, 1, 1)
            kept = 1.0 - 3.0 * diffusion
            for index, value in enumerate(
                (kept - last_sweep, stay, kept - next_sweep, last_sweep, sweep, next_sweep, over_sweep)
            ):
                winds[piece(7 * k + index, window, spot)] = value
            if k == 0:
                winds[piece(7 * levels, window, spot)] = begun[piece(fields + 3 * levels, window, spot)] + mask_share

    sub = lax.broadcasted_iota(jnp.int32, (EDGE, LANES), 0)

    def copies(cells, reach):
        out = {0: cells}
        for turn in range(1, reach + 1):
            out[turn] = [pltpu.roll(value, turn, 1) for value in cells]
            out[-turn] = [pltpu.roll(value, LANES - turn, 1) for value in cells]
        return out

    def carried_at(turned, k, backward, turn):
        cells, west, east = turned[turn], turned[turn + 1], turned[turn - 1]
        out = []
        for spot in spots:
            if spot:
                south = cells[spot - 1]
            else:
                south = jnp.where(sub == 0, 0.0, pltpu.roll(cells[-1], 1, 0))
            if spot < count - 1:
                north = cells[spot + 1]
            else:
                north = jnp.where(sub == EDGE - 1, 0.0, pltpu.roll(cells[0], EDGE - 1, 0))
            swept, other = (east[spot], west[spot]) if backward else (west[spot], east[spot])
            near = diffusion * ((north + south) + other)
            sweep = 7 * k + 4 + turn + (not backward)
            out.append(
                (near + winds[piece(7 * k + 1 + turn, window, spot)] * cells[spot])
                + winds[piece(sweep, window, spot)] * swept
            )
        return out

    def carried(cells, k, backward):
        return carried_at(copies(cells, 1), k, backward, 0)

    def each(function, *lists):
        return [function(*values) for values in zip(*lists)]

    def added(first, second):
        return each(lambda a, b: a + b, first, second)

    def total_of(lists):
        out = lists[0]
        for values in lists[1:]:
            out = added(out, values)
        return out

    def scaled(factor, values):
        return [factor * value for value in values]

    def more(base, factor, values):
        return each(lambda a, b: a + factor * b, base, values)

    sizes = range(bins)
    upper = [scales[size, :1] for size in sizes]
    lower = [scales[bins + size, :1] for size in sizes]

    def summed_forward(top, bottom):
        sunk = [[] for _ in range(3)]
        cells = top
        for index in range(3):
            sunk[index] = [scaled(upper[size], cells[size]) for size in sizes]
            if index < 2:
                cells = [each(lambda a, b: a - b, carried(cells[size], 0, False), sunk[index][size]) for size in sizes]
        turned, sinking = copies(total_of(cells), 2), copies(total_of(sunk[2]), 1)
        both = {
            turn: each(lambda a, b: a - b, carried_at(turned, 0, False, turn), sinking[turn]) for turn in (-1, 0, 1)
        }
        both = carried_at(both, 0, False, 0)
        factors = []
        for size in sizes:
            rate = -lower[size]
            first = scaled(rate, bottom[size])
            b3 = added(sunk[0][size], first)
            b2 = more(sunk[1][size], rate, b3)
            b1 = more(sunk[2][size], rate, b2)
            c0 = scaled(rate, b1)
            e3 = added(b3, first)
            e2 = more(b2, rate, e3)
            c1 = more(b1, rate, e2)
            f3 = added(e3, first)
            c2 = more(e2, rate, f3)
            c3 = added(f3, first)
            factors.append([c3, c2, c1, c0])
        moved = total_of(bottom)
        sums = [total_of([factor[index] for factor in factors]) for index in range(4)]
        for index in range(2):
            moved = added(carried(moved, 1, False), sums[index])
        turned, third = copies(moved, 2), copies(sums[2], 1)
        moved = {turn: added(carried_at(turned, 1, False, turn), third[turn]) for turn in (-1, 0, 1)}
        return added(both, added(carried_at(moved, 1, False, 0), sums[3]))

    def spread_backward(start):
        turned = copies(start, 2)
        lower_one, upper_one = (
            {turn: carried_at(turned, k, True, turn) for turn in (-1, 0, 1)} for k in (1, 0)
        )
        powers = [start, lower_one[0], carried_at(lower_one, 1, True, 0)]
        later = copies(powers[2], 2)
        lower_three = {turn: carried_at(later, 1, True, turn) for turn in (-1, 0, 1)}
        powers += [lower_three[0], carried_at(lower_three, 1, True, 0)]
        twice, thrice, thrice_more = scaled(2.0, powers[1]), scaled(3.0, powers[1]), scaled(3.0, powers[2])
        four, six, four_more = scaled(4.0, powers[1]), scaled(6.0, powers[2]), scaled(4.0, powers[3])
        first, second = upper_one[0], carried_at(upper_one, 0, True, 0)
        gap = each(lambda a, b: a - b, powers[1], first)
        third = carried(second, 0, True)
        next_gap = each(lambda a, b: a - b, carried_at(lower_one, 0, True, 0), second)
        tops, bottoms = [], []
        for size in sizes:
            rate = -lower[size]
            low_two = more(powers[2], rate, more(twice, rate, start))
            low_three = more(powers[3], rate, more(thrice_more, rate, more(thrice, rate, start)))
            low_four = more(powers[4], rate, more(four_more, rate, more(six, rate, more(four, rate, start))))
            cells = more(second, upper[size], more(gap, rate, start))
            gain = added(more(next_gap, rate, first), each(lambda a, b: a - b, low_two, cells))
            cells = more(third, upper[size], gain)
            gain = each(lambda a, b: a - b, low_three, cells)
            cells = more(carried(cells, 0, True), upper[size], gain)
            tops.append(cells)
            bottoms.append(low_four)
        return tops + bottoms

    scale = 1.0 / fields
    mask = [winds[piece(7 * levels, window, spot)] for spot in spots]
    for sweep in range(SWEEPS):
        cells = [[coarse[piece(field, window, spot)] for spot in spots] for field in range(fields)]
        if sweep:
            cells = [added(cells[field], [change[piece(field, window, spot)] for spot in spots]) for field in range(fields)]
        total = summed_forward(cells[:bins], cells[bins:])
        start = [
            rows_of(table, 0, window, spot) * (total[spot] * (scale * scale)) - rows_of(table, 1, window, spot) * scale
            for spot in spots
        ]
        adjoint = spread_backward(start)
        for field in range(fields):
            for spot in spots:
                if sweep:
                    old = change[piece(field, window, spot)]
                    value = old - step_length * (background * old + adjoint[field][spot])
                else:
                    value = -step_length * adjoint[field][spot]
                if sweep < SWEEPS - 1:
                    change[piece(field, window, spot)] = mask[spot] * value
                else:
                    coarse[pl.ds(field * window + spot, EDGE, stride=count), :] = mask[spot] * value

    final = [
        coarse[pl.ds(pl.multiple_of((level * bins + size) * window + own, 8), rows)] for size in range(bins)
    ]
    for size in range(bins):
        turned = final[size].T
        for slot in range(slots):
            start = slot * HALF + cols
            correction[slot, size, 0] = turned[start : start + cols]
    writes = [pltpu.make_async_copy(correction, correction_out, written.at[slots * bins])]
    writes[0].start()
    source_lane = lax.broadcasted_iota(jnp.int32, (LANES, slots * LANES), 0)
    target_lane = lax.broadcasted_iota(jnp.int32, (LANES, slots * LANES), 1)
    picks = source_lane == target_lane // LANES * HALF + cols + target_lane % LANES // BLOCK
    picks = picks.astype(jnp.float32).astype(jnp.bfloat16)
    wide = jnp.dot(
        three_parts(jnp.concatenate(final)), jnp.concatenate([picks] * 3), preferred_element_type=jnp.float32
    )
    growth = scales[levels * bins]
    fetch.wait()
    for slot in range(slots):
        for size in range(bins):
            cells = wide[size * rows : (size + 1) * rows, slot * LANES : (slot + 1) * LANES]
            raised = (cells[:, None, :] * growth[None]).reshape(rows * BLOCK, LANES)
            analysis[slot, size, 0] = (fine[slot, size, 0].astype(jnp.float32) + raised).astype(jnp.bfloat16)
            at = (slot, size)
            writes.append(pltpu.make_async_copy(analysis.at[at], analysis_out.at[at], written.at[slot * bins + size]))
            writes[-1].start()
    for write in writes:
        write.wait()


def solution(mesh):
    lon_count, lat_count, lev_count = (mesh.shape[axis] for axis in AXES)

    def place_of(lon, lat, lev):
        return (lon % lon_count * lat_count + lat) * lev_count + lev

    def moved(values, source_of):
        pairs = []
        for lon in range(lon_count):
            for lat in range(lat_count):
                for lev in range(lev_count):
                    source = source_of(lon, lat, lev)
                    if source is not None:
                        pairs.append((place_of(*source), place_of(lon, lat, lev)))
        return lax.ppermute(values, AXES, pairs)

    def per_device(
        trajectory,
        block_weights,
        wind_speed,
        settling,
        source_mask,
        obs_columns,
        obs_values,
        obs_weights,
    ):
        slots, bins, _, fine_rows, fine_cols = trajectory.shape
        rows, cols = fine_rows // BLOCK, fine_cols // BLOCK
        rims = min(lat_count - 1, 2)
        window = rows + rims * REACH
        small = pltpu.CompilerParams(vmem_limit_bytes=8 * 1024 * 1024)
        in_vmem = pl.BlockSpec(memory_space=pltpu.VMEM)

        def kept(array):
            return pltpu.with_memory_space_constraint(array, pltpu.HBM)

        in_hbm = pl.BlockSpec(memory_space=pltpu.HBM)

        def restrict(*refs):
            restrict_kernel(lat_count, slots, bins, rows, cols, *refs)

        packed = pl.pallas_call(
            restrict,
            out_shape=pltpu.VMEM((rows, LANES), jnp.float32),
            in_specs=[in_hbm] * 4,
            out_specs=in_vmem,
            scratch_shapes=[
                pltpu.VMEM(trajectory.shape, jnp.bfloat16),
                pltpu.VMEM((BLOCK, BLOCK), jnp.float32),
                pltpu.VMEM((1, cols, rows), jnp.float32),
                pltpu.VMEM((cols, rows), jnp.int32),
                pltpu.VMEM((slots * bins * fine_rows, LANES), jnp.float32),
                pltpu.SemaphoreType.DMA((3 + slots * bins,)),
            ],
            compiler_params=small,
        )(*map(kept, (trajectory, block_weights, wind_speed.swapaxes(1, 2), source_mask.T)))

        def tabulate(*refs):
            obs_kernel(lat_count, lon_count * cols, rows, cols, window, *refs)

        observed = (
            obs_columns.T,
            obs_values.swapaxes(1, 2),
            obs_weights.swapaxes(1, 2),
            settling.T,
            block_weights,
        )
        table, scales = pl.pallas_call(
            tabulate,
            out_shape=(
                pltpu.VMEM((2, window, LANES), jnp.float32),
                pltpu.VMEM((2 * bins + 1, BLOCK, LANES), jnp.float32),
            ),
            in_specs=[in_hbm] * 5,
            out_specs=(in_vmem, in_vmem),
            scratch_shapes=[pltpu.VMEM(array.shape, array.dtype) for array in observed]
            + [pltpu.SemaphoreType.DMA((5,))],
            compiler_params=small,
        )(*map(kept, observed))

        own = jnp.stack([packed, moved(packed, lambda lon, lat, lev: (lon, lat, 1 - lev))])
        near = moved(own, lambda lon, lat, lev: (lon ^ 1 if lev == 0 else lon + 1 - 2 * ((lon + 1) % 2), lat, lev))

        def rims_of(held):
            if lat_count == 2:
                return moved(held[:, :REACH], lambda lon, lat, lev: (lon, 1 - lat, lev))
            low = moved(
                held[:, rows - REACH :], lambda lon, lat, lev: (lon, lat - 1, lev) if lat > 0 else None
            )
            high = moved(
                held[:, :REACH], lambda lon, lat, lev: (lon, lat + 1, lev) if lat < lat_count - 1 else None
            )
            return jnp.concatenate([low, high], axis=1)

        own_rims, near_rims = lax.optimization_barrier((rims_of(own), rims_of(near)))
        near_rims, table, scales = lax.optimization_barrier((near_rims, table, scales))
        brought = jnp.concatenate([near.reshape(-1, LANES), near_rims.reshape(-1, LANES)])
        far = moved(brought, lambda lon, lat, lev: (lon, lat, 1 - lev))

        def cycle(*refs):
            cycle_kernel(lat_count, slots, bins, rows, cols, window, *refs)

        fields = 2 * bins
        fields = 2 * bins
        field_shape = ((fields + 7) * window, LANES)

        def unpack(*refs):
            unpack_kernel(lat_count, bins, rows, cols, window, *refs)

        begun = pl.pallas_call(
            unpack,
            out_shape=pltpu.VMEM(field_shape, jnp.float32),
            in_specs=[in_vmem] * 4,
            out_specs=in_vmem,
            scratch_shapes=[pltpu.VMEM((4 * window, LANES), jnp.float32)],
            compiler_params=small,
        )(own, near, own_rims, near_rims)
        begun, far = lax.optimization_barrier((begun, far))
        field_store = pltpu.VMEM((fields * window, LANES), jnp.float32)
        analysis, correction = pl.pallas_call(
            cycle,
            out_shape=(
                jax.ShapeDtypeStruct(trajectory.shape, jnp.bfloat16),
                jax.ShapeDtypeStruct((slots, bins, 1, cols, rows), jnp.float32),
            ),
            in_specs=[in_vmem] * 4 + [in_hbm],
            out_specs=(in_hbm, in_hbm),
            scratch_shapes=[
                pltpu.VMEM(trajectory.shape, jnp.bfloat16),
                pltpu.VMEM(trajectory.shape, jnp.bfloat16),
                pltpu.VMEM((slots, bins, 1, cols, rows), jnp.float32),
                field_store,
                field_store,
                pltpu.VMEM((15 * window, LANES), jnp.float32),
                pltpu.VMEM((2 * (bins + 3) * window, LANES), jnp.float32),
                pltpu.SemaphoreType.DMA,
                pltpu.SemaphoreType.DMA((slots * bins + 1,)),
            ],
            compiler_params=small,
        )(begun, far, table.reshape(-1, LANES), scales, kept(trajectory))
        return analysis, correction.swapaxes(3, 4)

    placed = (
        P("member", None, "lev", "lat", "lon"),
        P(),
        P("lev", "lat", "lon"),
        P(),
        P("lat", "lon"),
        P("member", None),
        P("member", None, None),
        P("member", None, None),
    )
    return jax.shard_map(
        per_device,
        mesh=mesh,
        in_specs=placed,
        out_specs=(P("member", None, "lev", "lat", "lon"), P("member", None, "lev", "lat", "lon")),
        check_vma=False,
    )
```
